256 devices in a mesh: gx: 8 (over z), gy: 4 (over x_lo, core), gz: 8 (over y, x_hi).
Axes of the slice: x: 4 (x_hi: 2, x_lo: 2; x = x_hi * 2 + x_lo), y: 4, z: 8, core: 2. Of those that a mesh axis runs over, the one named last changes fastest.
Arguments:
- volume: float32 [256, 256, 256], P('gx', ('gy', 'gz')), may hold values from -12 to 12
- prior_weight: float32 [256, 256, 256], P('gx', ('gy', 'gz')), may hold values from 0.1 to 2
- kernel: float32 [512, 512, 512], P(('gy', 'gz'), 'gx'), may hold values from 0.05 to 1
Outputs:
- hessian_product: float32 [256, 256, 256], P('gx', ('gy', 'gz'))
- curvature: float32 [1], replicated
The draws below stay inside these ranges and needn't reach their ends.
All inputs are finite; a program needn't handle non-finite values.
Results may differ from the reference program's by a relative error of at most 0.00005.
Values sent between devices are 32-bit elements; how exact they have to be, the bound alone decides.
No kernel may reach another device: no remote copies, remote signals or barrier semaphores. Data moves between devices by JAX's collectives and lax.ppermute only.
A program may use at most 64 MiB of HBM per device.

```python
import math
import jax
import jax.numpy as jnp

MAP = 256
GRID = 512


def draw_volume(key, part):
    key = jax.random.fold_in(key, 11)
    position = jnp.arange(MAP).astype(jnp.float32)
    ramp = 1.0 + 2.0 * position / float(MAP - 1)
    base = jnp.clip(jax.random.normal(key, (MAP, MAP, MAP), jnp.float32), -4.0, 4.0)
    return base * ramp[:, None, None]


def level_of(stream_key, shape, split, low, high):
    factor_of = 1.0
    for dim, shards_of in split:
        heights = jax.random.uniform(jax.random.fold_in(jax.random.fold_in(stream_key, 6), dim), (shards_of,), jnp.float32, low / len(split), high / len(split))
        factor_of = factor_of * jnp.repeat(jnp.exp(heights), shape[dim] // shards_of).reshape((-1,) + (1,) * (len(shape) - 1 - dim))
    return factor_of


def setup_inputs(seed: int = 0) -> dict:
    splits = jax.random.split(jax.random.key(seed), 4)
    return {
        "volume": draw_volume(jax.random.fold_in(splits[3], 71), 0),
        "prior_weight": jnp.clip(jnp.exp(math.log(2.0) - 2.9957323 * jax.random.uniform(splits[1], (MAP, MAP, MAP), jnp.float32) ** level_of(splits[1], (MAP, MAP, MAP), ((0, 8), (1, 32)), -0.2, 0.2)), 0.1, 2.0),
        "kernel": jnp.clip(jnp.exp(math.log(1.0) - 2.9957323 * jax.random.uniform(splits[2], (GRID, GRID, GRID), jnp.float32) ** level_of(splits[2], (GRID, GRID, GRID), ((0, 32), (1, 8)), -0.2, 0.2)), 0.05, 1.0),
    }


def reference(volume, prior_weight, kernel):
    size_m = volume.shape[0]
    size_n = 2 * size_m
    padded = jnp.zeros((size_n, size_n, size_n), volume.dtype)
    padded = padded.at[:size_m, :size_m, :size_m].set(volume)
    spectrum = jnp.fft.fftn(padded)
    weights = jnp.transpose(kernel, (0, 2, 1))
    weighted = spectrum * weights
    image = jnp.fft.ifftn(weighted)
    cropped = jnp.real(image[:size_m, :size_m, :size_m]).astype(volume.dtype)
    hessian_product = cropped + prior_weight * volume
    curvature = (jnp.sum(volume * hessian_product) / float(size_m) ** 3).reshape(1)
    return hessian_product, curvature
```

```python
import math

import jax
import jax.numpy as jnp
import ml_dtypes
import numpy as np
from jax import lax
from jax.experimental import pallas as pl
from jax.experimental.pallas import tpu as pltpu
from jax.sharding import PartitionSpec as P

M = 256
N = 512
GX = 8
GA = 32
BF = jnp.bfloat16
VMEM_LIMIT = 50 * 1024 * 1024


def trig(rows, cols):
    product = np.outer(np.asarray(rows), np.asarray(cols)) % N
    angle = product * (2.0 * math.pi / N)
    return np.cos(angle), np.sin(angle)


def halves(table):
    table = np.asarray(table, np.float32)
    high = table.astype(ml_dtypes.bfloat16)
    low = (table - high.astype(np.float32)).astype(ml_dtypes.bfloat16)
    return high, low


def z_forward_table():
    cosine, sine = trig(np.arange(M), np.arange(N))
    stacked = np.stack([cosine.reshape(M, GX, 64), -sine.reshape(M, GX, 64)], axis=2)
    return halves(stacked.reshape(M, GX * 128))


def x_forward_table():
    cosine, sine = trig(np.arange(N), np.arange(M))
    return halves(np.concatenate([cosine, sine], axis=1))


def y_inverse_table():
    cosine, sine = trig(np.arange(M), np.arange(N))
    return halves(np.concatenate([cosine, sine], axis=1))


def x_inverse_table():
    order = np.arange(N).reshape(GA, 16).T.reshape(-1)
    cosine, sine = trig(np.arange(M), order)
    return halves(np.concatenate([cosine, sine], axis=1))


def z_inverse_table():
    cosine, sine = trig(np.arange(N), np.arange(M))
    stacked = np.stack([cosine.reshape(GX, 64, M), -sine.reshape(GX, 64, M)], axis=1)
    return halves(stacked.reshape(GX * 128, M) / float(N) ** 3)


def split(value):
    high = value.astype(BF)
    low = (value - high.astype(jnp.float32)).astype(BF)
    return high, low


def dot(left, right):
    return jnp.dot(left, right, preferred_element_type=jnp.float32)


def dot3(left_high, left_low, right_high, right_low):
    return dot(left_high, right_high) + (dot(left_high, right_low) + dot(left_low, right_high))


def rotated(value, sign):
    lane = lax.broadcasted_iota(jnp.int32, value.shape, 1)
    swapped = pltpu.roll(value, 64, 1)
    return jnp.where(lane < 64, sign * swapped, -sign * swapped)


def fold(value):
    rows, cols = value.shape
    total = jnp.sum(value.reshape(rows // 8, 8, cols), axis=0)
    parts = [total[:, at : at + 128] for at in range(0, cols, 128)]
    return sum(parts[1:], parts[0])


def z_forward_kernel(volume, prior, high, low, out, partial):
    field = volume[...]
    partial[...] = fold((prior[...] * field * field).reshape(M, M))
    rows = jnp.concatenate([volume[:, y, :] for y in range(8)], axis=0)
    rows_high, rows_low = split(rows)
    for half in range(2):
        cols = slice(half * 512, half * 512 + 512)
        res = dot3(rows_high, rows_low, high[:, cols], low[:, cols])
        for block in range(4):
            out[half * 4 + block] = res[:, block * 128 : block * 128 + 128]


def x_forward_kernel(received, high, low, out):
    real = [received[:, y].reshape(M, 128) for y in range(2)]
    turned = [rotated(part, 1.0) for part in real]
    data = jnp.concatenate(
        [jnp.concatenate(real, axis=1), jnp.concatenate(turned, axis=1)], axis=0
    )
    data_high, data_low = split(data)
    res = dot3(high[...], low[...], data_high, data_low)
    for y in range(2):
        out[:, y] = res[:, y * 128 : y * 128 + 128].reshape(GA, 16, 128)


def y_kernel(received, weights, partial, fwd_high, fwd_low, inv_high, inv_low, out, total):
    step = pl.program_id(0)

    @pl.when(step == 0)
    def _():
        total[...] = jnp.zeros_like(total)

    real = [received[pl.ds(step * 2 + k, M, stride=16), :] for k in range(2)]
    turned = [rotated(part, 1.0) for part in real]
    data = jnp.concatenate(
        [jnp.concatenate(real, axis=1), jnp.concatenate(turned, axis=1)], axis=0
    )
    data_high, data_low = split(data)
    spectrum = dot3(fwd_high[...], fwd_low[...], data_high, data_low)
    scale = []
    for k in range(2):
        flipped = weights[k].T
        scale += [flipped, flipped]
    weighted = spectrum * jnp.concatenate(scale, axis=1)
    total[...] += fold(weighted * spectrum)
    back = jnp.concatenate(
        [rotated(weighted[:, :128], -1.0), rotated(weighted[:, 128:], -1.0)], axis=1
    )
    back_high, back_low = split(jnp.concatenate([weighted, back], axis=0))
    res = dot3(inv_high[...], inv_low[...], back_high, back_low)
    out[:, :, pl.ds(pl.multiple_of(step * 256, 256), 256)] = res.reshape(GA, 8, 256)

    @pl.when(step == 7)
    def _():
        count = total[...] * (1.0 / float(N) ** 3) + partial[...]
        out[:, :, 2048:] = jnp.broadcast_to(count[None], (GA, 8, 128))


def x_inverse_kernel(received, high, low, out):
    for pair in range(4):
        real = []
        for y in (2 * pair, 2 * pair + 1):
            real.append(
                jnp.concatenate(
                    [received[:, y, k * 128 : k * 128 + 128] for k in range(16)],
                    axis=0,
                )
            )
        turned = [rotated(part, -1.0) for part in real]
        data = jnp.concatenate(
            [jnp.concatenate(real, axis=1), jnp.concatenate(turned, axis=1)], axis=0
        )
        data_high, data_low = split(data)
        res = dot3(high[...], low[...], data_high, data_low)
        for at in range(2):
            y = 2 * pair + at
            out[:, y * 32 : y * 32 + 32, :] = res[:, at * 128 : at * 128 + 128].reshape(GX, 32, 128)
    group = jnp.sum(received[:, :, 2048:], axis=0)
    out[:, 256:, :] = jnp.broadcast_to(group[None], (GX, 8, 128))


def z_inverse_kernel(received, volume, prior, high, low, out, curvature):
    data = jnp.concatenate([received[c, :256, :] for c in range(GX)], axis=1)
    data_high, data_low = split(data)
    image = dot3(data_high, data_low, high[...], low[...])
    for y in range(8):
        out[:, y, :] = image[y * 32 : y * 32 + 32, :] + prior[:, y, :] * volume[:, y, :]
    total = jnp.sum(received[:, 256:, :], axis=0)
    curvature[...] = jnp.broadcast_to(jnp.sum(total) / float(M) ** 3, (8, 128))


def whole():
    return pl.BlockSpec(memory_space=pltpu.VMEM)


def params():
    return pltpu.CompilerParams(vmem_limit_bytes=VMEM_LIMIT)


def f32(*shape):
    return jax.ShapeDtypeStruct(shape, jnp.float32)


def local(volume, prior_weight, kernel):
    sent, partial = pl.pallas_call(
        z_forward_kernel,
        out_shape=(f32(GX, 256, 128), f32(8, 128)),
        in_specs=[whole()] * 4,
        out_specs=(whole(), whole()),
        compiler_params=params(),
        name="z_forward",
    )(volume, prior_weight, *z_forward_table())
    got = lax.all_to_all(sent, "gx", split_axis=0, concat_axis=0, tiled=True)
    sent = pl.pallas_call(
        x_forward_kernel,
        grid=(4,),
        out_shape=f32(GA, 8, 16, 128),
        in_specs=[pl.BlockSpec((GX, 2, 32, 128), lambda i: (0, i, 0, 0)), whole(), whole()],
        out_specs=pl.BlockSpec((GA, 2, 16, 128), lambda i: (0, i, 0, 0)),
        compiler_params=params(),
        name="x_forward",
    )(got.reshape(GX, 8, 32, 128), *x_forward_table())
    got = lax.all_to_all(sent, ("gy", "gz"), split_axis=0, concat_axis=0, tiled=True)
    sent = pl.pallas_call(
        y_kernel,
        grid=(8,),
        out_shape=f32(GA, 8, 2176),
        in_specs=[whole(), pl.BlockSpec((2, 64, 512), lambda i: (i, 0, 0))] + [whole()] * 5,
        out_specs=whole(),
        scratch_shapes=[pltpu.VMEM((8, 128), jnp.float32)],
        compiler_params=params(),
        name="y_both",
    )(got.reshape(GA * 8 * 16, 128), kernel, partial, *x_forward_table(), *y_inverse_table())
    got = lax.all_to_all(sent, ("gy", "gz"), split_axis=0, concat_axis=0, tiled=True)
    sent = pl.pallas_call(
        x_inverse_kernel,
        out_shape=f32(GX, 264, 128),
        in_specs=[whole()] * 3,
        out_specs=whole(),
        compiler_params=params(),
        name="x_inverse",
    )(got, *x_inverse_table())
    got = lax.all_to_all(sent, "gx", split_axis=0, concat_axis=0, tiled=True)
    product, curvature = pl.pallas_call(
        z_inverse_kernel,
        out_shape=(f32(32, 8, M), f32(8, 128)),
        in_specs=[whole()] * 5,
        out_specs=(whole(), whole()),
        compiler_params=params(),
        name="z_inverse",
    )(got, volume, prior_weight, *z_inverse_table())
    return product, curvature[0, :1]


def solution(mesh):
    return jax.shard_map(
        local,
        mesh=mesh,
        in_specs=(
            P("gx", ("gy", "gz"), None),
            P("gx", ("gy", "gz"), None),
            P(("gy", "gz"), "gx", None),
        ),
        out_specs=(P("gx", ("gy", "gz"), None), P()),
        check_vma=False,
    )
```

```python
import math

import jax
import jax.numpy as jnp
import ml_dtypes
import numpy as np
from jax import lax
from jax.experimental import pallas as pl
from jax.experimental.pallas import tpu as pltpu
from jax.sharding import PartitionSpec as P

M = 256
N = 512
GX = 8
GA = 32
HALF = 32
EARLY = 4
PACK_COST = 2
OWN_COST = 8
NEAR_COST = 20
FORWARD_COST = 5
AXES = ("gx", "gy", "gz")
BF = jnp.bfloat16
VMEM_LIMIT = 50 * 1024 * 1024


def trig(rows, cols):
    product = np.outer(np.asarray(rows), np.asarray(cols)) % N
    angle = product * (2.0 * math.pi / N)
    return np.cos(angle), np.sin(angle)


def halves(table):
    table = np.asarray(table, np.float32)
    high = table.astype(ml_dtypes.bfloat16)
    low = (table - high.astype(np.float32)).astype(ml_dtypes.bfloat16)
    return high, low


def z_forward_table():
    cosine, sine = trig(np.arange(M), np.arange(N))
    stacked = np.stack([cosine, -sine], axis=0).reshape(2, M, GX // 2, 2, 64)
    main = stacked[..., :HALF].transpose(1, 2, 0, 3, 4).reshape(M, GX * 64)
    edge = stacked[..., HALF].transpose(1, 2, 3, 0).reshape(M, GX * 2)
    return halves(np.concatenate([main, np.repeat(edge, 8, axis=1)], axis=1))


def z_inverse_table():
    cosine, sine = trig(np.arange(N), np.arange(M))
    stacked = np.stack([cosine, -sine], axis=0).reshape(2, GX // 2, 2, 64, M)
    main = stacked[:, :, :, :HALF].transpose(1, 0, 2, 3, 4).reshape(GX * 64, M)
    edge = stacked[:, :, :, HALF].transpose(1, 2, 0, 3).reshape(GX * 2, M)
    return halves(np.concatenate([main, np.repeat(edge, 8, axis=0)], axis=0) / float(N) ** 3)


def forward_table():
    cosine, sine = trig(np.arange(N), np.arange(M))
    return halves(np.concatenate([cosine, sine], axis=1))


def inverse_table():
    cosine, sine = trig(np.arange(M), np.arange(N))
    return halves(np.concatenate([cosine, sine], axis=1))


def x_inverse_table():
    order = np.arange(N).reshape(GA, 16).T.reshape(-1)
    cosine, sine = trig(np.arange(M), order)
    return halves(np.concatenate([cosine, sine], axis=1))


def flip_tables():
    flip = np.zeros((N, N), ml_dtypes.bfloat16)
    flip[np.arange(N), -np.arange(N) % N] = 1
    planes = np.zeros((128, 128), ml_dtypes.bfloat16)
    for block in range(0, 128, HALF):
        for at in range(1, HALF):
            planes[block + at, block + HALF - at] = 1
    return flip, planes


def split(value):
    high = value.astype(BF)
    low = (value - high.astype(jnp.float32)).astype(BF)
    return high, low


def dot(left, right):
    return jnp.dot(left, right, preferred_element_type=jnp.float32)


def dot3(left_high, left_low, right_high, right_low):
    return dot(left_high, right_high) + (dot(left_high, right_low) + dot(left_low, right_high))


def rotated(value, sign):
    lane = lax.broadcasted_iota(jnp.int32, value.shape, 1)
    swapped = pltpu.roll(value, 64, 1)
    return jnp.where(lane < 64, sign * swapped, -sign * swapped)


def fold(value):
    rows, cols = value.shape
    total = jnp.sum(value.reshape(rows // 8, 8, cols), axis=0)
    parts = [total[:, at : at + 128] for at in range(0, cols, 128)]
    return sum(parts[1:], parts[0])


def lanes(value):
    return lax.broadcasted_iota(jnp.int32, value.shape, value.ndim - 1)


def roll(value, shift):
    shift = shift % 128
    return value if shift == 0 else pltpu.roll(value, shift, value.ndim - 1)


def exchange(first, second):
    even = (lanes(first) & HALF) == 0
    low = jnp.where(even, first, roll(second, HALF))
    high = jnp.where(even, roll(first, -HALF), second)
    return low, high


def complex_dot(table_high, table_low, tiles, sign):
    real = jnp.concatenate(tiles, axis=1)
    turned = jnp.concatenate([rotated(tile, sign) for tile in tiles], axis=1)
    data_high, data_low = split(jnp.concatenate([real, turned], axis=0))
    return dot3(table_high[...], table_low[...], data_high, data_low)


def z_forward_kernel(volume, prior, high, low, out, partial):
    field = volume[...]
    partial[...] = fold((prior[...] * field * field).reshape(M, M))
    rows = jnp.concatenate([volume[:, y, :] for y in range(8)], axis=0)
    rows_high, rows_low = split(rows)
    res = dot3(rows_high, rows_low, high[...], low[...])
    for pair in range(GX // 2):
        tile = res[:, pair * 128 : pair * 128 + 128]
        first, second = exchange(tile[:128], tile[128:])
        out[2 * pair, :128] = first
        out[2 * pair + 1, :128] = second
    edge = res[:, GX * 64 :]
    lane = lax.broadcasted_iota(jnp.int32, (32, 128), 1)
    planes = jnp.zeros((32, 128), jnp.float32)
    for y in range(8):
        planes = jnp.where(lane % 8 == y, edge[y * 32 : y * 32 + 32], planes)
    lane = lax.broadcasted_iota(jnp.int32, (8, 128), 1)
    for block in range(GX):
        tile = jnp.zeros((8, 128), jnp.float32)
        for quarter in range(4):
            moved = roll(planes[quarter * 8 : quarter * 8 + 8], 16 * quarter - 16 * block)
            tile = jnp.where(lane // 16 == quarter, moved, tile)
        out[block, 128:] = tile


def x_forward_kernel(received, held, high, low, out):
    for pair in range(2):
        tiles = [
            received[:, y * 32 : y * 32 + 32, :].reshape(M, 128) for y in (2 * pair, 2 * pair + 1)
        ]
        res = complex_dot(high, low, tiles, 1.0)
        for at in range(2):
            blocks = res[:, at * 128 : at * 128 + 128].reshape(GA, 2, 8, 128)
            first, second = exchange(blocks[:, 0].reshape(M, 128), blocks[:, 1].reshape(M, 128))
            out[:, 2 * pair + at] = first.reshape(GA, 8, 128)
            out[:, 2 * pair + at + 4] = second.reshape(GA, 8, 128)
    lane = lax.broadcasted_iota(jnp.int32, (8, 128), 1)
    rows = []
    for block in range(GX):
        tile = received[block, 128:, :]
        for quarter in range(4):
            real = roll(tile, -16 * quarter)
            imag = roll(tile, 56 - 16 * quarter)
            rows.append(jnp.where(lane < 64, real, imag))
    res = complex_dot(high, low, [jnp.concatenate(rows, axis=0)], 1.0).T
    for group in range(GA):
        cols = slice(group // 8 * 128, group // 8 * 128 + 128)
        shift = -16 * (group % 8)
        out[group, 8] = jnp.where(
            lane < 64, roll(res[0:8, cols], shift), roll(res[64:72, cols], shift + 64)
        )


def doubled(tile):
    first, second = tile[:, :64], tile[:, 64:]
    return jnp.concatenate([first, first, second, second], axis=1)


def pair_order(pair):
    return 2 * pair, 2 * pair + 8, 2 * pair + 1, 2 * pair + 9


def flipped(rows, flip, planes):
    high, low = split(rows)
    turned_high, turned_low = split(dot(planes, high) + dot(planes, low))
    contract = (((1,), (1,)), ((), ()))
    return lax.dot_general(
        flip, turned_high, contract, preferred_element_type=jnp.float32
    ) + lax.dot_general(flip, turned_low, contract, preferred_element_type=jnp.float32)


def pack_kernel(plane, after, other, out):
    for k in range(EARLY + 1, 16):
        out[k - EARLY - 1] = plane[15 - k]


def own_kernel(own, after, out):
    for pair in range(4):
        rows = jnp.concatenate([own[k, :HALF] for k in pair_order(pair)], axis=0)
        out[:, pair * 256 : pair * 256 + 256] = doubled(rows.T)
    edge = jnp.concatenate([own[:, HALF, :], jnp.zeros((48, N), jnp.float32)] * 2, axis=0)
    out[:, 1024:] = edge.T


def near_kernel(base, near, rim, flip, planes, out):
    blank = jnp.zeros((HALF, N), jnp.float32)
    out[...] = base[...]
    for pair in range((EARLY + 2) // 2):
        place = slice(pair * 256, pair * 256 + 256)
        rows = [
            rim[0] if k == 0 else near[EARLY - k] if k <= EARLY else blank for k in pair_order(pair)
        ]
        out[:, place] += doubled(flipped(jnp.concatenate(rows, axis=0), flip[...], planes[...]))


def y_forward_kernel(received, high, low, out):
    for pair in range(4):
        tiles = []
        for at in range(2):
            rows = [
                received[pl.ds(group * 72 + pair * 2 + at, 8, stride=8), :] for group in range(GA)
            ]
            tiles.append(jnp.concatenate(rows, axis=0))
        out[:, pair * 256 : pair * 256 + 256] = complex_dot(high, low, tiles, 1.0)
    rows = [received[group * 72 + 64 : group * 72 + 72, :] for group in range(GA)]
    out[:, 1024:] = complex_dot(high, low, [jnp.concatenate(rows, axis=0)], 1.0)


def y_inverse_kernel(spectrum, base, far, partial, flip, planes, high, low, out):
    blank = jnp.zeros((HALF, N), jnp.float32)

    def mirrored(k):
        return far[k - EARLY - 1] if k > EARLY else blank

    total = partial[...]
    for pair in range(5):
        place = slice(pair * 256, min(pair * 256 + 256, 1152))
        scale = base[:, place]
        if pair < 4:
            rows = jnp.concatenate([mirrored(k) for k in pair_order(pair)], axis=0)
            scale += doubled(flipped(rows, flip[...], planes[...]))
        values = spectrum[:, place]
        weighted = values * scale
        total += fold(weighted * values) * (1.0 / float(N) ** 3)
        cols = [weighted[:, at : at + 128] for at in range(0, values.shape[1], 128)]
        res = complex_dot(high, low, cols, -1.0)
        if pair == 4:
            res = jnp.where(lanes(res) < 96, res, jnp.sum(total))
        out[:, :, place] = res.reshape(GA, 8, res.shape[1])


def x_inverse_kernel(received, high, low, plain_high, plain_low, out):
    for pair in range(2):
        tiles = []
        for y in (2 * pair, 2 * pair + 1):
            first, second = (
                jnp.concatenate(
                    [received[:, at, k * 128 : k * 128 + 128] for k in range(8)], axis=0
                )
                for at in (y, y + 4)
            )
            tiles.append(jnp.concatenate(exchange(first, second), axis=0))
        res = complex_dot(high, low, tiles, -1.0)
        for at in range(2):
            y = 2 * pair + at
            out[:, y * 32 : y * 32 + 32, :] = res[:, at * 128 : at * 128 + 128].reshape(GX, 32, 128)
    lane = lax.broadcasted_iota(jnp.int32, (8, 128), 1)
    real, imag = [], []
    count = jnp.zeros((1, 1), jnp.float32)
    for four in range(4):
        real_tile = jnp.zeros((8, 128), jnp.float32)
        imag_tile = real_tile
        for at in range(8):
            tile = received[four * 8 + at, :, 1024:]
            count += tile[:1, 127:]
            here = lane // 16 == at
            real_tile = jnp.where(here, roll(tile, 16 * at), real_tile)
            imag_tile = jnp.where(here, roll(tile, 16 * at - 64), imag_tile)
        real.append(real_tile)
        imag.append(imag_tile)
    blank = jnp.zeros((56, N), jnp.float32)
    stacked = jnp.concatenate(
        [jnp.concatenate(real, axis=1), blank, jnp.concatenate(imag, axis=1), blank], axis=0
    )
    res = complex_dot(plain_high, plain_low, [stacked.T], -1.0)
    for block in range(GX):
        tile = jnp.broadcast_to(count, (8, 128))
        for quarter in range(4):
            part = res[block * 32 + quarter * 8 : block * 32 + quarter * 8 + 8]
            tile = jnp.where(lane // 8 == 2 * quarter, roll(part, 16 * quarter), tile)
            tile = jnp.where(lane // 8 == 2 * quarter + 1, roll(part, 16 * quarter - 56), tile)
        out[block, 128:] = tile


def z_inverse_kernel(received, volume, prior, high, low, out, curvature):
    lower, upper = [], []
    for pair in range(GX // 2):
        first, second = exchange(received[2 * pair, :128], received[2 * pair + 1, :128])
        lower.append(first)
        upper.append(second)
    lane = lax.broadcasted_iota(jnp.int32, (8, 128), 1)
    planes = []
    for quarter in range(4):
        tile = jnp.zeros((8, 128), jnp.float32)
        for block in range(GX):
            moved = roll(received[block, 128:], 16 * block - 16 * quarter)
            tile = jnp.where(lane // 16 == block, moved, tile)
        planes.append(tile)
    planes = jnp.concatenate(planes, axis=0)
    edge = jnp.concatenate(
        [jnp.where(lanes(planes) % 8 == y, planes, 0.0) for y in range(8)], axis=0
    )
    main = jnp.concatenate(
        [jnp.concatenate(lower, axis=1), jnp.concatenate(upper, axis=1)], axis=0
    )
    data_high, data_low = split(jnp.concatenate([main, edge], axis=1))
    image = dot3(data_high, data_low, high[...], low[...])
    for y in range(8):
        out[:, y, :] = image[y * 32 : y * 32 + 32, :] + prior[:, y, :] * volume[:, y, :]
    total = jnp.sum(received[:, 128:, 127:].reshape(GX * 8, 1)) / 8.0
    curvature[0] = total / float(M) ** 3


def whole():
    return pl.BlockSpec(memory_space=pltpu.VMEM)


def params():
    return pltpu.CompilerParams(vmem_limit_bytes=VMEM_LIMIT)


def cost(micros):
    return pl.CostEstimate(flops=int(micros * 1e9), bytes_accessed=8 << 20, transcendentals=0)


def f32(*shape):
    return jax.ShapeDtypeStruct(shape, jnp.float32)


def mirror(value, shift):
    pairs = [((shift - group) % GA, group) for group in range(GA)]
    return lax.ppermute(value, ("gy", "gz"), pairs)


def opposite(value):
    return lax.ppermute(value, "gx", [(GX - 1 - block, block) for block in range(GX)])


def local(volume, prior_weight, kernel):
    flips = flip_tables()
    turned = opposite(kernel[16 - EARLY :, HALF:])
    near = mirror(turned, 31)
    plane = mirror(kernel[1 : 16 - EARLY, HALF:], 31)
    rim = opposite(mirror(kernel[:1, HALF:], 32))
    base = pl.pallas_call(
        own_kernel,
        out_shape=f32(N, 1152),
        in_specs=[whole(), pl.BlockSpec(memory_space=pl.ANY)],
        out_specs=whole(),
        compiler_params=params(),
        cost_estimate=cost(OWN_COST),
        name="own_weights",
    )(kernel, turned)
    sent, partial = pl.pallas_call(
        z_forward_kernel,
        out_shape=(f32(GX, 136, 128), f32(8, 128)),
        in_specs=[whole()] * 4,
        out_specs=(whole(), whole()),
        compiler_params=params(),
        name="z_forward",
    )(volume, prior_weight, *z_forward_table())
    got = lax.all_to_all(sent, "gx", split_axis=0, concat_axis=0, tiled=True)
    packed = pl.pallas_call(
        pack_kernel,
        out_shape=f32(15 - EARLY, HALF, N),
        in_specs=[whole()] + [pl.BlockSpec(memory_space=pl.ANY)] * 2,
        out_specs=whole(),
        compiler_params=params(),
        cost_estimate=cost(PACK_COST),
        name="pack",
    )(plane, got, base)
    far = opposite(packed)
    sent = pl.pallas_call(
        x_forward_kernel,
        out_shape=f32(GA, 9, 8, 128),
        in_specs=[whole(), pl.BlockSpec(memory_space=pl.ANY), whole(), whole()],
        out_specs=whole(),
        compiler_params=params(),
        name="x_forward",
    )(got, packed, *forward_table())
    got = lax.all_to_all(sent, ("gy", "gz"), split_axis=0, concat_axis=0, tiled=True)
    base = pl.pallas_call(
        near_kernel,
        out_shape=f32(N, 1152),
        in_specs=[whole()] * 5,
        out_specs=whole(),
        compiler_params=params(),
        cost_estimate=cost(NEAR_COST),
        name="near_weights",
    )(base, near, rim, *flips)
    spectrum = pl.pallas_call(
        y_forward_kernel,
        out_shape=f32(N, 1152),
        in_specs=[whole()] * 3,
        out_specs=whole(),
        compiler_params=params(),
        cost_estimate=cost(FORWARD_COST),
        name="y_forward",
    )(got.reshape(GA * 72, 128), *forward_table())
    sent = pl.pallas_call(
        y_inverse_kernel,
        out_shape=f32(GA, 8, 1152),
        in_specs=[whole()] * 8,
        out_specs=whole(),
        compiler_params=params(),
        name="y_inverse",
    )(spectrum, base, far, partial, *flips, *inverse_table())
    got = lax.all_to_all(sent, ("gy", "gz"), split_axis=0, concat_axis=0, tiled=True)
    sent = pl.pallas_call(
        x_inverse_kernel,
        out_shape=f32(GX, 136, 128),
        in_specs=[whole()] * 5,
        out_specs=whole(),
        compiler_params=params(),
        name="x_inverse",
    )(got, *x_inverse_table(), *inverse_table())
    got = lax.all_to_all(sent, "gx", split_axis=0, concat_axis=0, tiled=True)
    product, curvature = pl.pallas_call(
        z_inverse_kernel,
        out_shape=(f32(32, 8, M), f32(1)),
        in_specs=[whole()] * 5,
        out_specs=(whole(), pl.BlockSpec(memory_space=pltpu.SMEM)),
        compiler_params=params(),
        name="z_inverse",
    )(got, volume, prior_weight, *z_inverse_table())
    return product, curvature


def solution(mesh):
    return jax.shard_map(
        local,
        mesh=mesh,
        in_specs=(
            P("gx", ("gy", "gz"), None),
            P("gx", ("gy", "gz"), None),
            P(("gy", "gz"), "gx", None),
        ),
        out_specs=(P("gx", ("gy", "gz"), None), P()),
        check_vma=False,
    )
```

```python
import math

import jax
import jax.numpy as jnp
import ml_dtypes
import numpy as np
from jax import lax
from jax.experimental import pallas as pl
from jax.experimental.pallas import tpu as pltpu
from jax.sharding import PartitionSpec as P

M = 256
N = 512
GX = 8
GA = 32
HALF = 32
EARLY = 6
LATE = 15 - EARLY
OWN_COST = 20
TURN_COST = 8
FORWARD_COST = 5
AXES = ("gx", "gy", "gz")
VM = 32
BF = jnp.bfloat16


def trig(rows, cols):
    product = np.outer(np.asarray(rows), np.asarray(cols)) % N
    angle = product * (2.0 * math.pi / N)
    return np.cos(angle), np.sin(angle)


def halves(table):
    table = np.asarray(table, np.float32)
    high = table.astype(ml_dtypes.bfloat16)
    low = (table - high.astype(np.float32)).astype(ml_dtypes.bfloat16)
    return high, low


def z_forward_table():
    cosine, sine = trig(np.arange(M), np.arange(N))
    stacked = np.stack([cosine, -sine], axis=0).reshape(2, M, GX // 2, 2, 64)
    main = stacked[..., :HALF].transpose(1, 2, 0, 3, 4).reshape(M, GX * 64)
    edge = stacked[..., HALF].transpose(1, 2, 3, 0).reshape(M, GX * 2)
    return np.concatenate(halves(np.concatenate([main, np.repeat(edge, 8, axis=1)], axis=1)), axis=0)


def z_inverse_table():
    cosine, sine = trig(np.arange(N), np.arange(M))
    stacked = np.stack([cosine, -sine], axis=0).reshape(2, GX // 2, 2, 64, M)
    main = stacked[:, :, :, :HALF].transpose(1, 0, 2, 3, 4).reshape(GX * 64, M)
    edge = stacked[:, :, :, HALF].transpose(1, 2, 0, 3).reshape(GX * 2, M)
    return stack_right(np.concatenate([main, np.repeat(edge, 8, axis=0)], axis=0) / float(N) ** 3)


def forward_table():
    cosine, sine = trig(np.arange(N), np.arange(M))
    return stack_left(np.concatenate([cosine, sine], axis=1))


def inverse_table():
    cosine, sine = trig(np.arange(M), np.arange(N))
    return stack_left(np.concatenate([cosine, sine], axis=1))


def x_inverse_table():
    order = np.arange(N).reshape(GA, 16).T.reshape(-1)
    cosine, sine = trig(np.arange(M), order)
    return stack_left(np.concatenate([cosine, sine], axis=1))


def split(value):
    high = value.astype(BF)
    low = (value - high.astype(jnp.float32)).astype(BF)
    return high, low


def dot(left, right):
    return jnp.dot(left, right, preferred_element_type=jnp.float32)


def stack_left(table):
    return np.concatenate(halves(table), axis=1)


def stack_right(table):
    high, low = halves(table)
    return np.concatenate([high, low, high], axis=0)


def table_dot(table, data):
    high, low = split(data)
    depth = data.shape[0]
    return dot(table[...], jnp.concatenate([high, high], axis=0)) + dot(table[:, :depth], low)


def data_dot(data, table):
    high, low = split(data)
    return dot(jnp.concatenate([high, high, low], axis=1), table[...])


def rotated(value, sign):
    lane = lax.broadcasted_iota(jnp.int32, value.shape, 1)
    swapped = pltpu.roll(value, 64, 1)
    return jnp.where(lane < 64, sign * swapped, -sign * swapped)


def fold(value):
    rows, cols = value.shape
    total = jnp.sum(value.reshape(rows // 8, 8, cols), axis=0)
    parts = [total[:, at : at + 128] for at in range(0, cols, 128)]
    return sum(parts[1:], parts[0])


def lanes(value):
    return lax.broadcasted_iota(jnp.int32, value.shape, value.ndim - 1)


def roll(value, shift):
    shift = shift % 128
    return value if shift == 0 else pltpu.roll(value, shift, value.ndim - 1)


def exchange(first, second):
    even = (lanes(first) & HALF) == 0
    low = jnp.where(even, first, roll(second, HALF))
    high = jnp.where(even, roll(first, -HALF), second)
    return low, high


def complex_dot(table, tiles, sign):
    real = jnp.concatenate(tiles, axis=1)
    turned = jnp.concatenate([rotated(tile, sign) for tile in tiles], axis=1)
    return table_dot(table, jnp.concatenate([real, turned], axis=0))


def z_forward_kernel(volume, table, out, field, held, sems):
    copies = []
    for part in range(4):
        place = pl.ds(part * 8, 8)
        copies.append(pltpu.make_async_copy(volume.at[place], field.at[place], sems.at[part]))
    for part in range(4):
        place = pl.ds(part * 128, 128)
        copies.append(pltpu.make_async_copy(table.at[place], held.at[place], sems.at[4 + part]))
    for copy in copies:
        copy.start()
    for copy in copies[:4]:
        copy.wait()
    high, low = split(jnp.concatenate([field[:, y, :] for y in range(8)], axis=0))
    for copy in copies[4:]:
        copy.wait()
    res = dot(jnp.concatenate([high, low], axis=0), held[:M])
    res = res[:M] + (res[M:] + dot(high, held[M:]))
    for pair in range(GX // 2):
        tile = res[:, pair * 128 : pair * 128 + 128]
        first, second = exchange(tile[:128], tile[128:])
        out[2 * pair, :128] = first
        out[2 * pair + 1, :128] = second
    edge = res[:, GX * 64 :]
    lane = lax.broadcasted_iota(jnp.int32, (32, 128), 1)
    planes = jnp.zeros((32, 128), jnp.float32)
    for y in range(8):
        planes = jnp.where(lane % 8 == y, edge[y * 32 : y * 32 + 32], planes)
    lane = lax.broadcasted_iota(jnp.int32, (8, 128), 1)
    for block in range(GX):
        tile = jnp.zeros((8, 128), jnp.float32)
        for quarter in range(4):
            moved = roll(planes[quarter * 8 : quarter * 8 + 8], 16 * quarter - 16 * block)
            tile = jnp.where(lane // 16 == quarter, moved, tile)
        out[block, 128:] = tile


def x_forward_kernel(received, held, table, out):
    for pair in range(2):
        tiles = [
            received[:, y * 32 : y * 32 + 32, :].reshape(M, 128) for y in (2 * pair, 2 * pair + 1)
        ]
        res = complex_dot(table, tiles, 1.0)
        for at in range(2):
            blocks = res[:, at * 128 : at * 128 + 128].reshape(GA, 2, 8, 128)
            first, second = exchange(blocks[:, 0].reshape(M, 128), blocks[:, 1].reshape(M, 128))
            out[:, 2 * pair + at] = first.reshape(GA, 8, 128)
            out[:, 2 * pair + at + 4] = second.reshape(GA, 8, 128)
    lane = lax.broadcasted_iota(jnp.int32, (8, 128), 1)
    rows = []
    for block in range(GX):
        tile = received[block, 128:, :]
        for quarter in range(4):
            real = roll(tile, -16 * quarter)
            imag = roll(tile, 56 - 16 * quarter)
            rows.append(jnp.where(lane < 64, real, imag))
    res = complex_dot(table, [jnp.concatenate(rows, axis=0)], 1.0).T
    for group in range(GA):
        cols = slice(group // 8 * 128, group // 8 * 128 + 128)
        shift = -16 * (group % 8)
        out[group, 8] = jnp.where(
            lane < 64, roll(res[0:8, cols], shift), roll(res[64:72, cols], shift + 64)
        )


def doubled(tile):
    first, second = tile[:, :64], tile[:, 64:]
    return jnp.concatenate([first, first, second, second], axis=1)


def pair_order(pair):
    return 2 * pair, 2 * pair + 8, 2 * pair + 1, 2 * pair + 9


def flipped(rows):
    shape = (128, 128)
    at, source = (lax.broadcasted_iota(jnp.int32, shape, axis) for axis in (0, 1))
    planes = (at // HALF == source // HALF) & (at % HALF + source % HALF == HALF)
    planes = jnp.where(planes, 1.0, 0.0).astype(BF)
    at, source = (lax.broadcasted_iota(jnp.int32, (N, N), axis) for axis in (0, 1))
    flip = jnp.where((at + source) % N == 0, 1.0, 0.0).astype(BF)
    count = rows.shape[0]
    high, low = [], []
    for first in range(0, count, 128):
        block = dot(planes, jnp.concatenate(split(rows[first : first + 128]), axis=1))
        upper, lower = split(block[:, :N] + block[:, N:])
        high.append(upper)
        low.append(lower)
    res = dot(jnp.concatenate(high + low, axis=0), flip)
    return res[:count] + res[count:]


def turn_kernel(own, late, early, rows, sems):
    copies = [
        pltpu.make_async_copy(own.at[k, pl.ds(HALF, HALF)], rows.at[k], sems.at[k])
        for k in range(16)
    ]
    for copy in copies:
        copy.start()
    for copy in copies:
        copy.wait()
    res = flipped(jnp.concatenate([rows[(16 - k) % 16] for k in range(1, 17)], axis=0))
    res = res.reshape(16, HALF, N)
    early[:EARLY] = res[:EARLY]
    early[EARLY:] = res[15:]
    late[...] = res[EARLY:15]


def own_kernel(own, volume, prior, out, partial):
    field = volume[...]
    partial[...] = fold((prior[...] * field * field).reshape(M, M))
    for pair in range(4):
        rows = jnp.concatenate([own[k, :HALF] for k in pair_order(pair)], axis=0)
        out[:, pair * 256 : pair * 256 + 256] = doubled(rows.T)
    edge = jnp.concatenate([own[:, HALF, :], jnp.zeros((48, N), jnp.float32)] * 2, axis=0)
    out[:, 1024:] = edge.T


def y_forward_kernel(received, table, out):
    for pair in range(4):
        tiles = []
        for at in range(2):
            rows = [
                received[pl.ds(group * 72 + pair * 2 + at, 8, stride=8), :] for group in range(GA)
            ]
            tiles.append(jnp.concatenate(rows, axis=0))
        out[:, pair * 256 : pair * 256 + 256] = complex_dot(table, tiles, 1.0)
    rows = [received[group * 72 + 64 : group * 72 + 72, :] for group in range(GA)]
    out[:, 1024:] = complex_dot(table, [jnp.concatenate(rows, axis=0)], 1.0)


def y_inverse_kernel(spectrum, base, far, near, rim, partial, table, out):
    def extra(pair):
        rows = [
            far[k - EARLY - 1] if k > EARLY else near[k - 1] if k else rim[0]
            for k in pair_order(pair)
        ]
        return doubled(jnp.concatenate(rows, axis=0).T)

    total = partial[...]
    for pair in range(5):
        place = slice(pair * 256, min(pair * 256 + 256, 1152))
        scale = base[:, place]
        if pair < 4:
            scale += extra(pair)
        values = spectrum[:, place]
        weighted = values * scale
        total += fold(weighted * values) * (1.0 / float(N) ** 3)
        cols = [weighted[:, at : at + 128] for at in range(0, values.shape[1], 128)]
        res = complex_dot(table, cols, -1.0)
        if pair == 4:
            res = jnp.where(lanes(res) < 96, res, jnp.sum(total))
        out[:, :, place] = res.reshape(GA, 8, res.shape[1])


def x_inverse_kernel(received, table, plain, out):
    for pair in range(2):
        tiles = []
        for y in (2 * pair, 2 * pair + 1):
            first, second = (
                jnp.concatenate(
                    [received[:, at, k * 128 : k * 128 + 128] for k in range(8)], axis=0
                )
                for at in (y, y + 4)
            )
            tiles.append(jnp.concatenate(exchange(first, second), axis=0))
        res = complex_dot(table, tiles, -1.0)
        for at in range(2):
            y = 2 * pair + at
            out[:, y * 32 : y * 32 + 32, :] = res[:, at * 128 : at * 128 + 128].reshape(GX, 32, 128)
    lane = lax.broadcasted_iota(jnp.int32, (8, 128), 1)
    real, imag = [], []
    count = jnp.zeros((1, 1), jnp.float32)
    for four in range(4):
        real_tile = jnp.zeros((8, 128), jnp.float32)
        imag_tile = real_tile
        for at in range(8):
            tile = received[four * 8 + at, :, 1024:]
            count += tile[:1, 127:]
            here = lane // 16 == at
            real_tile = jnp.where(here, roll(tile, 16 * at), real_tile)
            imag_tile = jnp.where(here, roll(tile, 16 * at - 64), imag_tile)
        real.append(real_tile)
        imag.append(imag_tile)
    blank = jnp.zeros((56, N), jnp.float32)
    stacked = jnp.concatenate(
        [jnp.concatenate(real, axis=1), blank, jnp.concatenate(imag, axis=1), blank], axis=0
    )
    res = complex_dot(plain, [stacked.T], -1.0)
    for block in range(GX):
        tile = jnp.broadcast_to(count, (8, 128))
        for quarter in range(4):
            part = res[block * 32 + quarter * 8 : block * 32 + quarter * 8 + 8]
            tile = jnp.where(lane // 8 == 2 * quarter, roll(part, 16 * quarter), tile)
            tile = jnp.where(lane // 8 == 2 * quarter + 1, roll(part, 16 * quarter - 56), tile)
        out[block, 128:] = tile


def z_inverse_kernel(received, volume, prior, table, out, curvature):
    lower, upper = [], []
    for pair in range(GX // 2):
        first, second = exchange(received[2 * pair, :128], received[2 * pair + 1, :128])
        lower.append(first)
        upper.append(second)
    lane = lax.broadcasted_iota(jnp.int32, (8, 128), 1)
    planes = []
    for quarter in range(4):
        tile = jnp.zeros((8, 128), jnp.float32)
        for block in range(GX):
            moved = roll(received[block, 128:], 16 * block - 16 * quarter)
            tile = jnp.where(lane // 16 == block, moved, tile)
        planes.append(tile)
    planes = jnp.concatenate(planes, axis=0)
    edge = jnp.concatenate(
        [jnp.where(lanes(planes) % 8 == y, planes, 0.0) for y in range(8)], axis=0
    )
    main = jnp.concatenate(
        [jnp.concatenate(lower, axis=1), jnp.concatenate(upper, axis=1)], axis=0
    )
    image = data_dot(jnp.concatenate([main, edge], axis=1), table)
    for y in range(8):
        out[:, y, :] = image[y * 32 : y * 32 + 32, :] + prior[:, y, :] * volume[:, y, :]
    total = jnp.sum(received[:, 128:, 127:].reshape(GX * 8, 1)) / 8.0
    curvature[0] = total / float(M) ** 3


def whole():
    return pl.BlockSpec(memory_space=pltpu.VMEM)


def anywhere():
    return pl.BlockSpec(memory_space=pl.ANY)


def in_hbm():
    return pl.BlockSpec(memory_space=pltpu.HBM)


def params(limit=VM):
    return pltpu.CompilerParams(vmem_limit_bytes=limit * 1024 * 1024)


def cost(micros):
    return pl.CostEstimate(flops=int(micros * 1e9), bytes_accessed=8 << 20, transcendentals=0)


def f32(*shape):
    return jax.ShapeDtypeStruct(shape, jnp.float32)


def mirror(value):
    pairs = [(GA - 1 - group, group) for group in range(GA)]
    return lax.ppermute(value, ("gy", "gz"), pairs)


def onward(value):
    return lax.ppermute(value, ("gy", "gz"), [(group, (group + 1) % GA) for group in range(GA)])


def reflect(value):
    count = GX * GA
    return lax.ppermute(value, AXES, [(count - 1 - at, at) for at in range(count)])


def opposite(value):
    return lax.ppermute(value, "gx", [(GX - 1 - block, block) for block in range(GX)])


def local(volume, prior_weight, kernel):
    late, early = pl.pallas_call(
        turn_kernel,
        out_shape=(f32(LATE, HALF, N), f32(EARLY + 1, HALF, N)),
        in_specs=[in_hbm()],
        out_specs=(whole(), whole()),
        scratch_shapes=[pltpu.VMEM((16, HALF, N), jnp.float32), pltpu.SemaphoreType.DMA((16,))],
        compiler_params=params(63),
        cost_estimate=cost(TURN_COST),
        name="turn",
    )(kernel)
    plane = mirror(late)
    near = reflect(early)
    rim = onward(near[EARLY:])
    base, partial = pl.pallas_call(
        own_kernel,
        out_shape=(f32(N, 1152), f32(8, 128)),
        in_specs=[whole()] * 3,
        out_specs=(whole(), whole()),
        compiler_params=params(),
        cost_estimate=cost(OWN_COST),
        name="own_weights",
    )(kernel, volume, prior_weight)
    sent = pl.pallas_call(
        z_forward_kernel,
        out_shape=f32(GX, 136, 128),
        in_specs=[in_hbm()] * 2,
        out_specs=whole(),
        scratch_shapes=[
            pltpu.VMEM((32, 8, M), jnp.float32),
            pltpu.VMEM((2 * M, 640), BF),
            pltpu.SemaphoreType.DMA((8,)),
        ],
        compiler_params=params(63),
        name="z_forward",
    )(volume, z_forward_table())
    got = lax.all_to_all(sent, "gx", split_axis=0, concat_axis=0, tiled=True)
    far = opposite(plane)
    sent = pl.pallas_call(
        x_forward_kernel,
        out_shape=f32(GA, 9, 8, 128),
        in_specs=[whole(), anywhere(), whole()],
        out_specs=whole(),
        compiler_params=params(),
        name="x_forward",
    )(got, plane, forward_table())
    got = lax.all_to_all(sent, ("gy", "gz"), split_axis=0, concat_axis=0, tiled=True)
    spectrum = pl.pallas_call(
        y_forward_kernel,
        out_shape=f32(N, 1152),
        in_specs=[whole()] * 2,
        out_specs=whole(),
        compiler_params=params(),
        cost_estimate=cost(FORWARD_COST),
        name="y_forward",
    )(got.reshape(GA * 72, 128), forward_table())
    sent = pl.pallas_call(
        y_inverse_kernel,
        out_shape=f32(GA, 8, 1152),
        in_specs=[whole()] * 7,
        out_specs=whole(),
        compiler_params=params(),
        name="y_inverse",
    )(spectrum, base, far, near, rim, partial, inverse_table())
    got = lax.all_to_all(sent, ("gy", "gz"), split_axis=0, concat_axis=0, tiled=True)
    sent = pl.pallas_call(
        x_inverse_kernel,
        out_shape=f32(GX, 136, 128),
        in_specs=[whole()] * 3,
        out_specs=whole(),
        compiler_params=params(),
        name="x_inverse",
    )(got, x_inverse_table(), inverse_table())
    got = lax.all_to_all(sent, "gx", split_axis=0, concat_axis=0, tiled=True)
    product, curvature = pl.pallas_call(
        z_inverse_kernel,
        out_shape=(f32(32, 8, M), f32(1)),
        in_specs=[whole()] * 4,
        out_specs=(whole(), pl.BlockSpec(memory_space=pltpu.SMEM)),
        compiler_params=params(),
        name="z_inverse",
    )(got, volume, prior_weight, z_inverse_table())
    return product, curvature


def solution(mesh):
    return jax.shard_map(
        local,
        mesh=mesh,
        in_specs=(
            P("gx", ("gy", "gz"), None),
            P("gx", ("gy", "gz"), None),
            P(("gy", "gz"), "gx", None),
        ),
        out_specs=(P("gx", ("gy", "gz"), None), P()),
        check_vma=False,
    )
```

```python
import math

import jax
import jax.numpy as jnp
import ml_dtypes
import numpy as np
from jax import lax
from jax.experimental import pallas as pl
from jax.experimental.pallas import tpu as pltpu
from jax.sharding import PartitionSpec as P

M = 256
N = 512
GX = 8
GA = 32
HALF = 32
EARLY = 6
LATE = 15 - EARLY
OWN_COST = 20
TURN_COST = 8
FORWARD_COST = 5
AXES = ("gx", "gy", "gz")
VM = 32
BF = jnp.bfloat16


def trig(rows, cols):
    product = np.outer(np.asarray(rows), np.asarray(cols)) % N
    angle = product * (2.0 * math.pi / N)
    return np.cos(angle), np.sin(angle)


def halves(table):
    table = np.asarray(table, np.float32)
    high = table.astype(ml_dtypes.bfloat16)
    low = (table - high.astype(np.float32)).astype(ml_dtypes.bfloat16)
    return high, low


def z_forward_table():
    cosine, sine = trig(np.arange(M), np.arange(N))
    stacked = np.stack([cosine, -sine], axis=0).reshape(2, M, GX // 2, 2, 64)
    main = stacked[..., :HALF].transpose(1, 2, 0, 3, 4).reshape(M, GX * 64)
    edge = stacked[..., HALF].transpose(1, 2, 3, 0).reshape(M, GX * 2)
    return np.concatenate(halves(np.concatenate([main, np.repeat(edge, 8, axis=1)], axis=1)), axis=0)


def z_inverse_table():
    cosine, sine = trig(np.arange(N), np.arange(M))
    stacked = np.stack([cosine, -sine], axis=0).reshape(2, GX // 2, 2, 64, M)
    main = stacked[:, :, :, :HALF].transpose(1, 0, 2, 3, 4).reshape(GX * 64, M)
    edge = stacked[:, :, :, HALF].transpose(1, 2, 0, 3).reshape(GX * 2, M)
    return stack_right(np.concatenate([main, np.repeat(edge, 8, axis=0)], axis=0) / float(N) ** 3)


def forward_table():
    cosine, sine = trig(np.arange(N), np.arange(M))
    return stack_left(np.concatenate([cosine, sine], axis=1))


def inverse_table():
    cosine, sine = trig(np.arange(M), np.arange(N))
    return stack_left(np.concatenate([cosine, sine], axis=1))


def x_inverse_table():
    order = np.arange(N).reshape(GA, 16).T.reshape(-1)
    cosine, sine = trig(np.arange(M), order)
    return stack_left(np.concatenate([cosine, sine], axis=1))


def split(value):
    high = value.astype(BF)
    low = (value - high.astype(jnp.float32)).astype(BF)
    return high, low


def dot(left, right):
    return jnp.dot(left, right, preferred_element_type=jnp.float32)


def stack_left(table):
    return np.concatenate(halves(table), axis=0)


def stack_right(table):
    high, low = halves(table)
    return np.concatenate([high, low, high], axis=0)


def table_dot(table, data):
    high, low = split(data)
    count = table.shape[0] // 2
    wide = dot(table[...], high)
    return wide[:count] + (wide[count:] + dot(table[:count], low))


def data_dot(data, table):
    high, low = split(data)
    return dot(jnp.concatenate([high, high, low], axis=1), table[...])


def rotated(value, sign):
    lane = lax.broadcasted_iota(jnp.int32, value.shape, 1)
    swapped = pltpu.roll(value, 64, 1)
    return jnp.where(lane < 64, sign * swapped, -sign * swapped)


def fold(value):
    rows, cols = value.shape
    total = jnp.sum(value.reshape(rows // 8, 8, cols), axis=0)
    parts = [total[:, at : at + 128] for at in range(0, cols, 128)]
    return sum(parts[1:], parts[0])


def lanes(value):
    return lax.broadcasted_iota(jnp.int32, value.shape, value.ndim - 1)


def roll(value, shift):
    shift = shift % 128
    return value if shift == 0 else pltpu.roll(value, shift, value.ndim - 1)


def exchange(first, second):
    even = (lanes(first) & HALF) == 0
    low = jnp.where(even, first, roll(second, HALF))
    high = jnp.where(even, roll(first, -HALF), second)
    return low, high


def complex_dot(table, tiles, sign):
    real = jnp.concatenate(tiles, axis=1)
    turned = jnp.concatenate([rotated(tile, sign) for tile in tiles], axis=1)
    return table_dot(table, jnp.concatenate([real, turned], axis=0))


def z_forward_kernel(volume, table, out, field, held, sems):
    copies = []
    for part in range(4):
        place = pl.ds(part * 8, 8)
        copies.append(pltpu.make_async_copy(volume.at[place], field.at[place], sems.at[part]))
    for part in range(4):
        place = pl.ds(part * 128, 128)
        copies.append(pltpu.make_async_copy(table.at[place], held.at[place], sems.at[4 + part]))
    for copy in copies:
        copy.start()
    for copy in copies[:4]:
        copy.wait()
    high, low = split(jnp.concatenate([field[:, y, :] for y in range(8)], axis=0))
    for copy in copies[4:]:
        copy.wait()
    res = dot(jnp.concatenate([high, low], axis=0), held[:M])
    res = res[:M] + (res[M:] + dot(high, held[M:]))
    for pair in range(GX // 2):
        tile = res[:, pair * 128 : pair * 128 + 128]
        first, second = exchange(tile[:128], tile[128:])
        out[2 * pair, :128] = first
        out[2 * pair + 1, :128] = second
    edge = res[:, GX * 64 :]
    lane = lax.broadcasted_iota(jnp.int32, (32, 128), 1)
    planes = jnp.zeros((32, 128), jnp.float32)
    for y in range(8):
        planes = jnp.where(lane % 8 == y, edge[y * 32 : y * 32 + 32], planes)
    lane = lax.broadcasted_iota(jnp.int32, (8, 128), 1)
    for block in range(GX):
        tile = jnp.zeros((8, 128), jnp.float32)
        for quarter in range(4):
            moved = roll(planes[quarter * 8 : quarter * 8 + 8], 16 * quarter - 16 * block)
            tile = jnp.where(lane // 16 == quarter, moved, tile)
        out[block, 128:] = tile


def x_forward_kernel(received, held, table, out):
    for pair in range(2):
        tiles = [
            received[:, y * 32 : y * 32 + 32, :].reshape(M, 128) for y in (2 * pair, 2 * pair + 1)
        ]
        res = complex_dot(table, tiles, 1.0)
        for at in range(2):
            blocks = res[:, at * 128 : at * 128 + 128].reshape(GA, 2, 8, 128)
            first, second = exchange(blocks[:, 0].reshape(M, 128), blocks[:, 1].reshape(M, 128))
            out[:, 2 * pair + at] = first.reshape(GA, 8, 128)
            out[:, 2 * pair + at + 4] = second.reshape(GA, 8, 128)
    lane = lax.broadcasted_iota(jnp.int32, (8, 128), 1)
    rows = []
    for block in range(GX):
        tile = received[block, 128:, :]
        for quarter in range(4):
            real = roll(tile, -16 * quarter)
            imag = roll(tile, 56 - 16 * quarter)
            rows.append(jnp.where(lane < 64, real, imag))
    res = complex_dot(table, [jnp.concatenate(rows, axis=0)], 1.0).T
    for group in range(GA):
        cols = slice(group // 8 * 128, group // 8 * 128 + 128)
        shift = -16 * (group % 8)
        out[group, 8] = jnp.where(
            lane < 64, roll(res[0:8, cols], shift), roll(res[64:72, cols], shift + 64)
        )


def doubled(tile):
    first, second = tile[:, :64], tile[:, 64:]
    return jnp.concatenate([first, first, second, second], axis=1)


def pair_order(pair):
    return 2 * pair, 2 * pair + 8, 2 * pair + 1, 2 * pair + 9


def flipped(rows):
    shape = (128, 128)
    at, source = (lax.broadcasted_iota(jnp.int32, shape, axis) for axis in (0, 1))
    planes = (at // HALF == source // HALF) & (at % HALF + source % HALF == HALF)
    planes = jnp.where(planes, 1.0, 0.0).astype(BF)
    at, source = (lax.broadcasted_iota(jnp.int32, (N, N), axis) for axis in (0, 1))
    flip = jnp.where((at + source) % N == 0, 1.0, 0.0).astype(BF)
    count = rows.shape[0]
    high, low = [], []
    for first in range(0, count, 128):
        block = dot(planes, jnp.concatenate(split(rows[first : first + 128]), axis=1))
        upper, lower = split(block[:, :N] + block[:, N:])
        high.append(upper)
        low.append(lower)
    res = dot(jnp.concatenate(high + low, axis=0), flip)
    return res[:count] + res[count:]


def turn_kernel(own, late, early, rows, sems):
    copies = [
        pltpu.make_async_copy(own.at[k, pl.ds(HALF, HALF)], rows.at[k], sems.at[k])
        for k in range(16)
    ]
    for copy in copies:
        copy.start()
    for copy in copies:
        copy.wait()
    res = flipped(jnp.concatenate([rows[(16 - k) % 16] for k in range(1, 17)], axis=0))
    res = res.reshape(16, HALF, N)
    early[:EARLY] = res[:EARLY]
    early[EARLY:] = res[15:]
    late[...] = res[EARLY:15]


def own_kernel(own, volume, prior, out, partial):
    field = volume[...]
    partial[...] = fold((prior[...] * field * field).reshape(M, M))
    for pair in range(4):
        rows = jnp.concatenate([own[k, :HALF] for k in pair_order(pair)], axis=0)
        out[:, pair * 256 : pair * 256 + 256] = doubled(rows.T)
    edge = jnp.concatenate([own[:, HALF, :], jnp.zeros((48, N), jnp.float32)] * 2, axis=0)
    out[:, 1024:] = edge.T


def y_forward_kernel(received, table, out):
    for pair in range(4):
        tiles = []
        for at in range(2):
            rows = [
                received[pl.ds(group * 72 + pair * 2 + at, 8, stride=8), :] for group in range(GA)
            ]
            tiles.append(jnp.concatenate(rows, axis=0))
        out[:, pair * 256 : pair * 256 + 256] = complex_dot(table, tiles, 1.0)
    rows = [received[group * 72 + 64 : group * 72 + 72, :] for group in range(GA)]
    out[:, 1024:] = complex_dot(table, [jnp.concatenate(rows, axis=0)], 1.0)


def y_inverse_kernel(spectrum, base, far, near, rim, partial, table, out):
    def extra(pair):
        rows = [
            far[k - EARLY - 1] if k > EARLY else near[k - 1] if k else rim[0]
            for k in pair_order(pair)
        ]
        return doubled(jnp.concatenate(rows, axis=0).T)

    total = partial[...]
    for pair in range(5):
        place = slice(pair * 256, min(pair * 256 + 256, 1152))
        scale = base[:, place]
        if pair < 4:
            scale += extra(pair)
        values = spectrum[:, place]
        weighted = values * scale
        total += fold(weighted * values) * (1.0 / float(N) ** 3)
        cols = [weighted[:, at : at + 128] for at in range(0, values.shape[1], 128)]
        res = complex_dot(table, cols, -1.0)
        if pair == 4:
            res = jnp.where(lanes(res) < 96, res, jnp.sum(total))
        out[:, :, place] = res.reshape(GA, 8, res.shape[1])


def x_inverse_kernel(received, table, plain, out):
    for pair in range(2):
        tiles = []
        for y in (2 * pair, 2 * pair + 1):
            first, second = (
                jnp.concatenate(
                    [received[:, at, k * 128 : k * 128 + 128] for k in range(8)], axis=0
                )
                for at in (y, y + 4)
            )
            tiles.append(jnp.concatenate(exchange(first, second), axis=0))
        res = complex_dot(table, tiles, -1.0)
        for at in range(2):
            y = 2 * pair + at
            out[:, y * 32 : y * 32 + 32, :] = res[:, at * 128 : at * 128 + 128].reshape(GX, 32, 128)
    lane = lax.broadcasted_iota(jnp.int32, (8, 128), 1)
    real, imag = [], []
    count = jnp.zeros((1, 1), jnp.float32)
    for four in range(4):
        real_tile = jnp.zeros((8, 128), jnp.float32)
        imag_tile = real_tile
        for at in range(8):
            tile = received[four * 8 + at, :, 1024:]
            count += tile[:1, 127:]
            here = lane // 16 == at
            real_tile = jnp.where(here, roll(tile, 16 * at), real_tile)
            imag_tile = jnp.where(here, roll(tile, 16 * at - 64), imag_tile)
        real.append(real_tile)
        imag.append(imag_tile)
    blank = jnp.zeros((56, N), jnp.float32)
    stacked = jnp.concatenate(
        [jnp.concatenate(real, axis=1), blank, jnp.concatenate(imag, axis=1), blank], axis=0
    )
    res = complex_dot(plain, [stacked.T], -1.0)
    for block in range(GX):
        tile = jnp.broadcast_to(count, (8, 128))
        for quarter in range(4):
            part = res[block * 32 + quarter * 8 : block * 32 + quarter * 8 + 8]
            tile = jnp.where(lane // 8 == 2 * quarter, roll(part, 16 * quarter), tile)
            tile = jnp.where(lane // 8 == 2 * quarter + 1, roll(part, 16 * quarter - 56), tile)
        out[block, 128:] = tile


def z_inverse_kernel(received, volume, prior, table, out, curvature):
    lower, upper = [], []
    for pair in range(GX // 2):
        first, second = exchange(received[2 * pair, :128], received[2 * pair + 1, :128])
        lower.append(first)
        upper.append(second)
    lane = lax.broadcasted_iota(jnp.int32, (8, 128), 1)
    planes = []
    for quarter in range(4):
        tile = jnp.zeros((8, 128), jnp.float32)
        for block in range(GX):
            moved = roll(received[block, 128:], 16 * block - 16 * quarter)
            tile = jnp.where(lane // 16 == block, moved, tile)
        planes.append(tile)
    planes = jnp.concatenate(planes, axis=0)
    edge = jnp.concatenate(
        [jnp.where(lanes(planes) % 8 == y, planes, 0.0) for y in range(8)], axis=0
    )
    main = jnp.concatenate(
        [jnp.concatenate(lower, axis=1), jnp.concatenate(upper, axis=1)], axis=0
    )
    image = data_dot(jnp.concatenate([main, edge], axis=1), table)
    for y in range(8):
        out[:, y, :] = image[y * 32 : y * 32 + 32, :] + prior[:, y, :] * volume[:, y, :]
    total = jnp.sum(received[:, 128:, 127:].reshape(GX * 8, 1)) / 8.0
    curvature[0] = total / float(M) ** 3


def whole():
    return pl.BlockSpec(memory_space=pltpu.VMEM)


def anywhere():
    return pl.BlockSpec(memory_space=pl.ANY)


def in_hbm():
    return pl.BlockSpec(memory_space=pltpu.HBM)


def params(limit=VM):
    return pltpu.CompilerParams(vmem_limit_bytes=limit * 1024 * 1024)


def cost(micros):
    return pl.CostEstimate(flops=int(micros * 1e9), bytes_accessed=8 << 20, transcendentals=0)


def f32(*shape):
    return jax.ShapeDtypeStruct(shape, jnp.float32)


def mirror(value):
    pairs = [(GA - 1 - group, group) for group in range(GA)]
    return lax.ppermute(value, ("gy", "gz"), pairs)


def onward(value):
    return lax.ppermute(value, ("gy", "gz"), [(group, (group + 1) % GA) for group in range(GA)])


def reflect(value):
    count = GX * GA
    return lax.ppermute(value, AXES, [(count - 1 - at, at) for at in range(count)])


def opposite(value):
    return lax.ppermute(value, "gx", [(GX - 1 - block, block) for block in range(GX)])


def local(volume, prior_weight, kernel):
    late, early = pl.pallas_call(
        turn_kernel,
        out_shape=(f32(LATE, HALF, N), f32(EARLY + 1, HALF, N)),
        in_specs=[in_hbm()],
        out_specs=(whole(), whole()),
        scratch_shapes=[pltpu.VMEM((16, HALF, N), jnp.float32), pltpu.SemaphoreType.DMA((16,))],
        compiler_params=params(63),
        cost_estimate=cost(TURN_COST),
        name="turn",
    )(kernel)
    plane = mirror(late)
    near = reflect(early)
    rim = onward(near[EARLY:])
    base, partial = pl.pallas_call(
        own_kernel,
        out_shape=(f32(N, 1152), f32(8, 128)),
        in_specs=[whole()] * 3,
        out_specs=(whole(), whole()),
        compiler_params=params(),
        cost_estimate=cost(OWN_COST),
        name="own_weights",
    )(kernel, volume, prior_weight)
    sent = pl.pallas_call(
        z_forward_kernel,
        out_shape=f32(GX, 136, 128),
        in_specs=[in_hbm()] * 2,
        out_specs=whole(),
        scratch_shapes=[
            pltpu.VMEM((32, 8, M), jnp.float32),
            pltpu.VMEM((2 * M, 640), BF),
            pltpu.SemaphoreType.DMA((8,)),
        ],
        compiler_params=params(63),
        name="z_forward",
    )(volume, z_forward_table())
    got = lax.all_to_all(sent, "gx", split_axis=0, concat_axis=0, tiled=True)
    far = opposite(plane)
    sent = pl.pallas_call(
        x_forward_kernel,
        out_shape=f32(GA, 9, 8, 128),
        in_specs=[whole(), anywhere(), whole()],
        out_specs=whole(),
        compiler_params=params(),
        name="x_forward",
    )(got, plane, forward_table())
    got = lax.all_to_all(sent, ("gy", "gz"), split_axis=0, concat_axis=0, tiled=True)
    spectrum = pl.pallas_call(
        y_forward_kernel,
        out_shape=f32(N, 1152),
        in_specs=[whole()] * 2,
        out_specs=whole(),
        compiler_params=params(),
        cost_estimate=cost(FORWARD_COST),
        name="y_forward",
    )(got.reshape(GA * 72, 128), forward_table())
    sent = pl.pallas_call(
        y_inverse_kernel,
        out_shape=f32(GA, 8, 1152),
        in_specs=[whole()] * 7,
        out_specs=whole(),
        compiler_params=params(),
        name="y_inverse",
    )(spectrum, base, far, near, rim, partial, inverse_table())
    got = lax.all_to_all(sent, ("gy", "gz"), split_axis=0, concat_axis=0, tiled=True)
    sent = pl.pallas_call(
        x_inverse_kernel,
        out_shape=f32(GX, 136, 128),
        in_specs=[whole()] * 3,
        out_specs=whole(),
        compiler_params=params(),
        name="x_inverse",
    )(got, x_inverse_table(), inverse_table())
    got = lax.all_to_all(sent, "gx", split_axis=0, concat_axis=0, tiled=True)
    product, curvature = pl.pallas_call(
        z_inverse_kernel,
        out_shape=(f32(32, 8, M), f32(1)),
        in_specs=[whole()] * 4,
        out_specs=(whole(), pl.BlockSpec(memory_space=pltpu.SMEM)),
        compiler_params=params(),
        name="z_inverse",
    )(got, volume, prior_weight, z_inverse_table())
    return product, curvature


def solution(mesh):
    return jax.shard_map(
        local,
        mesh=mesh,
        in_specs=(
            P("gx", ("gy", "gz"), None),
            P("gx", ("gy", "gz"), None),
            P(("gy", "gz"), "gx", None),
        ),
        out_specs=(P("gx", ("gy", "gz"), None), P()),
        check_vma=False,
    )
```

```python
import math

import jax
import jax.numpy as jnp
import ml_dtypes
import numpy as np
from jax import lax
from jax.experimental import pallas as pl
from jax.experimental.pallas import tpu as pltpu
from jax.sharding import PartitionSpec as P

M = 256
N = 512
GX = 8
GA = 32
HALF = 32
EARLY = 6
LATE = 15 - EARLY
OWN_COST = 20
TURN_COST = 8
FORWARD_COST = 5
AXES = ("gx", "gy", "gz")
VM = 32
BF = jnp.bfloat16


def trig(rows, cols):
    product = np.outer(np.asarray(rows), np.asarray(cols)) % N
    angle = product * (2.0 * math.pi / N)
    return np.cos(angle), np.sin(angle)


def halves(table):
    table = np.asarray(table, np.float32)
    high = table.astype(ml_dtypes.bfloat16)
    low = (table - high.astype(np.float32)).astype(ml_dtypes.bfloat16)
    return high, low


def z_forward_table():
    cosine, sine = trig(np.arange(M), np.arange(N))
    stacked = np.stack([cosine, -sine], axis=0).reshape(2, M, GX // 2, 2, 64)
    main = stacked[..., :HALF].transpose(1, 2, 0, 3, 4).reshape(M, GX * 64)
    edge = stacked[..., HALF].transpose(1, 2, 3, 0).reshape(M, GX * 2)
    return np.concatenate(halves(np.concatenate([main, np.repeat(edge, 8, axis=1)], axis=1)), axis=0)


def z_inverse_table():
    cosine, sine = trig(np.arange(N), np.arange(M))
    stacked = np.stack([cosine, -sine], axis=0).reshape(2, GX // 2, 2, 64, M)
    main = stacked[:, :, :, :HALF].transpose(1, 0, 2, 3, 4).reshape(GX * 64, M)
    edge = stacked[:, :, :, HALF].transpose(1, 2, 0, 3).reshape(GX * 2, M)
    return stack_left(np.concatenate([main, np.repeat(edge, 8, axis=0)], axis=0) / float(N) ** 3)


def forward_table():
    cosine, sine = trig(np.arange(N), np.arange(M))
    return stack_left(np.concatenate([cosine, sine], axis=1))


def inverse_table():
    cosine, sine = trig(np.arange(M), np.arange(N))
    return stack_left(np.concatenate([cosine, sine], axis=1))


def x_inverse_table():
    order = np.arange(N).reshape(GA, 16).T.reshape(-1)
    cosine, sine = trig(np.arange(M), order)
    return stack_left(np.concatenate([cosine, sine], axis=1))


def split(value):
    high = value.astype(BF)
    low = (value - high.astype(jnp.float32)).astype(BF)
    return high, low


def dot(left, right):
    return jnp.dot(left, right, preferred_element_type=jnp.float32)


def stack_left(table):
    return np.concatenate(halves(table), axis=0)


def table_dot(table, data):
    high, low = split(data)
    count = table.shape[0] // 2
    wide = dot(table[...], high)
    return wide[:count] + (wide[count:] + dot(table[:count], low))


def data_dot(data, table):
    high, low = split(data)
    count, depth = data.shape
    wide = dot(jnp.concatenate([high, low], axis=0), table[:depth])
    return wide[:count] + (wide[count:] + dot(high, table[depth:]))


def rotated(value, sign):
    lane = lax.broadcasted_iota(jnp.int32, value.shape, 1)
    swapped = pltpu.roll(value, 64, 1)
    return jnp.where(lane < 64, sign * swapped, -sign * swapped)


def fold(value):
    rows, cols = value.shape
    total = jnp.sum(value.reshape(rows // 8, 8, cols), axis=0)
    parts = [total[:, at : at + 128] for at in range(0, cols, 128)]
    return sum(parts[1:], parts[0])


def lanes(value):
    return lax.broadcasted_iota(jnp.int32, value.shape, value.ndim - 1)


def roll(value, shift):
    shift = shift % 128
    return value if shift == 0 else pltpu.roll(value, shift, value.ndim - 1)


def exchange(first, second):
    even = (lanes(first) & HALF) == 0
    low = jnp.where(even, first, roll(second, HALF))
    high = jnp.where(even, roll(first, -HALF), second)
    return low, high


def complex_dot(table, tiles, sign):
    real = jnp.concatenate(tiles, axis=1)
    turned = jnp.concatenate([rotated(tile, sign) for tile in tiles], axis=1)
    return table_dot(table, jnp.concatenate([real, turned], axis=0))


def z_forward_kernel(volume, table, out, field, held, sems):
    copies = []
    for part in range(4):
        place = pl.ds(part * 8, 8)
        copies.append(pltpu.make_async_copy(volume.at[place], field.at[place], sems.at[part]))
    for part in range(4):
        place = pl.ds(part * 128, 128)
        copies.append(pltpu.make_async_copy(table.at[place], held.at[place], sems.at[4 + part]))
    for copy in copies:
        copy.start()
    for copy in copies[:4]:
        copy.wait()
    high, low = split(jnp.concatenate([field[:, y, :] for y in range(8)], axis=0))
    for copy in copies[4:]:
        copy.wait()
    res = dot(jnp.concatenate([high, low], axis=0), held[:M])
    res = res[:M] + (res[M:] + dot(high, held[M:]))
    for pair in range(GX // 2):
        tile = res[:, pair * 128 : pair * 128 + 128]
        first, second = exchange(tile[:128], tile[128:])
        out[2 * pair, :128] = first
        out[2 * pair + 1, :128] = second
    edge = res[:, GX * 64 :]
    lane = lax.broadcasted_iota(jnp.int32, (32, 128), 1)
    planes = jnp.zeros((32, 128), jnp.float32)
    for y in range(8):
        planes = jnp.where(lane % 8 == y, edge[y * 32 : y * 32 + 32], planes)
    lane = lax.broadcasted_iota(jnp.int32, (8, 128), 1)
    for block in range(GX):
        tile = jnp.zeros((8, 128), jnp.float32)
        for quarter in range(4):
            moved = roll(planes[quarter * 8 : quarter * 8 + 8], 16 * quarter - 16 * block)
            tile = jnp.where(lane // 16 == quarter, moved, tile)
        out[block, 128:] = tile


def x_forward_kernel(received, held, table, out):
    for pair in range(2):
        tiles = [
            received[:, y * 32 : y * 32 + 32, :].reshape(M, 128) for y in (2 * pair, 2 * pair + 1)
        ]
        res = complex_dot(table, tiles, 1.0)
        for at in range(2):
            blocks = res[:, at * 128 : at * 128 + 128].reshape(GA, 2, 8, 128)
            first, second = exchange(blocks[:, 0].reshape(M, 128), blocks[:, 1].reshape(M, 128))
            out[:, 2 * pair + at] = first.reshape(GA, 8, 128)
            out[:, 2 * pair + at + 4] = second.reshape(GA, 8, 128)
    lane = lax.broadcasted_iota(jnp.int32, (8, 128), 1)
    rows = []
    for block in range(GX):
        tile = received[block, 128:, :]
        for quarter in range(4):
            real = roll(tile, -16 * quarter)
            imag = roll(tile, 56 - 16 * quarter)
            rows.append(jnp.where(lane < 64, real, imag))
    res = complex_dot(table, [jnp.concatenate(rows, axis=0)], 1.0).T
    for group in range(GA):
        cols = slice(group // 8 * 128, group // 8 * 128 + 128)
        shift = -16 * (group % 8)
        out[group, 8] = jnp.where(
            lane < 64, roll(res[0:8, cols], shift), roll(res[64:72, cols], shift + 64)
        )


def doubled(tile):
    first, second = tile[:, :64], tile[:, 64:]
    return jnp.concatenate([first, first, second, second], axis=1)


def pair_order(pair):
    return 2 * pair, 2 * pair + 8, 2 * pair + 1, 2 * pair + 9


def flipped(rows):
    shape = (128, 128)
    at, source = (lax.broadcasted_iota(jnp.int32, shape, axis) for axis in (0, 1))
    planes = (at // HALF == source // HALF) & (at % HALF + source % HALF == HALF)
    planes = jnp.where(planes, 1.0, 0.0).astype(BF)
    at, source = (lax.broadcasted_iota(jnp.int32, (N, N), axis) for axis in (0, 1))
    flip = jnp.where((at + source) % N == 0, 1.0, 0.0).astype(BF)
    count = rows.shape[0]
    high, low = [], []
    for first in range(0, count, 128):
        block = dot(planes, jnp.concatenate(split(rows[first : first + 128]), axis=1))
        upper, lower = split(block[:, :N] + block[:, N:])
        high.append(upper)
        low.append(lower)
    res = dot(jnp.concatenate(high + low, axis=0), flip)
    return res[:count] + res[count:]


def turn_kernel(own, late, early, rows, sems):
    copies = [
        pltpu.make_async_copy(own.at[k, pl.ds(HALF, HALF)], rows.at[k], sems.at[k])
        for k in range(16)
    ]
    for copy in copies:
        copy.start()
    for copy in copies:
        copy.wait()
    res = flipped(jnp.concatenate([rows[(16 - k) % 16] for k in range(1, 17)], axis=0))
    res = res.reshape(16, HALF, N)
    early[:EARLY] = res[:EARLY]
    early[EARLY:] = res[15:]
    late[...] = res[EARLY:15]


def own_kernel(own, volume, prior, out, partial):
    field = volume[...]
    partial[...] = fold((prior[...] * field * field).reshape(M, M))
    for pair in range(4):
        rows = jnp.concatenate([own[k, :HALF] for k in pair_order(pair)], axis=0)
        out[:, pair * 256 : pair * 256 + 256] = doubled(rows.T)
    edge = jnp.concatenate([own[:, HALF, :], jnp.zeros((48, N), jnp.float32)] * 2, axis=0)
    out[:, 1024:] = edge.T


def y_forward_kernel(received, table, out):
    for pair in range(4):
        tiles = []
        for at in range(2):
            rows = [
                received[pl.ds(group * 72 + pair * 2 + at, 8, stride=8), :] for group in range(GA)
            ]
            tiles.append(jnp.concatenate(rows, axis=0))
        out[:, pair * 256 : pair * 256 + 256] = complex_dot(table, tiles, 1.0)
    rows = [received[group * 72 + 64 : group * 72 + 72, :] for group in range(GA)]
    out[:, 1024:] = complex_dot(table, [jnp.concatenate(rows, axis=0)], 1.0)


def y_inverse_kernel(spectrum, base, far, near, rim, partial, table, out):
    def extra(pair):
        rows = [
            far[k - EARLY - 1] if k > EARLY else near[k - 1] if k else rim[0]
            for k in pair_order(pair)
        ]
        return doubled(jnp.concatenate(rows, axis=0).T)

    total = partial[...]
    for pair in range(5):
        place = slice(pair * 256, min(pair * 256 + 256, 1152))
        scale = base[:, place]
        if pair < 4:
            scale += extra(pair)
        values = spectrum[:, place]
        weighted = values * scale
        total += fold(weighted * values) * (1.0 / float(N) ** 3)
        cols = [weighted[:, at : at + 128] for at in range(0, values.shape[1], 128)]
        res = complex_dot(table, cols, -1.0)
        if pair == 4:
            res = jnp.where(lanes(res) < 96, res, jnp.sum(total))
        out[:, :, place] = res.reshape(GA, 8, res.shape[1])


def x_inverse_kernel(received, table, plain, out):
    for pair in range(2):
        tiles = []
        for y in (2 * pair, 2 * pair + 1):
            first, second = (
                jnp.concatenate(
                    [received[:, at, k * 128 : k * 128 + 128] for k in range(8)], axis=0
                )
                for at in (y, y + 4)
            )
            tiles.append(jnp.concatenate(exchange(first, second), axis=0))
        res = complex_dot(table, tiles, -1.0)
        for at in range(2):
            y = 2 * pair + at
            out[:, y * 32 : y * 32 + 32, :] = res[:, at * 128 : at * 128 + 128].reshape(GX, 32, 128)
    lane = lax.broadcasted_iota(jnp.int32, (8, 128), 1)
    real, imag = [], []
    count = jnp.zeros((1, 1), jnp.float32)
    for four in range(4):
        real_tile = jnp.zeros((8, 128), jnp.float32)
        imag_tile = real_tile
        for at in range(8):
            tile = received[four * 8 + at, :, 1024:]
            count += tile[:1, 127:]
            here = lane // 16 == at
            real_tile = jnp.where(here, roll(tile, 16 * at), real_tile)
            imag_tile = jnp.where(here, roll(tile, 16 * at - 64), imag_tile)
        real.append(real_tile)
        imag.append(imag_tile)
    blank = jnp.zeros((56, N), jnp.float32)
    stacked = jnp.concatenate(
        [jnp.concatenate(real, axis=1), blank, jnp.concatenate(imag, axis=1), blank], axis=0
    )
    res = complex_dot(plain, [stacked.T], -1.0)
    for block in range(GX):
        tile = jnp.broadcast_to(count, (8, 128))
        for quarter in range(4):
            part = res[block * 32 + quarter * 8 : block * 32 + quarter * 8 + 8]
            tile = jnp.where(lane // 8 == 2 * quarter, roll(part, 16 * quarter), tile)
            tile = jnp.where(lane // 8 == 2 * quarter + 1, roll(part, 16 * quarter - 56), tile)
        out[block, 128:] = tile


def z_inverse_kernel(received, volume, prior, table, out, curvature):
    lower, upper = [], []
    for pair in range(GX // 2):
        first, second = exchange(received[2 * pair, :128], received[2 * pair + 1, :128])
        lower.append(first)
        upper.append(second)
    lane = lax.broadcasted_iota(jnp.int32, (8, 128), 1)
    planes = []
    for quarter in range(4):
        tile = jnp.zeros((8, 128), jnp.float32)
        for block in range(GX):
            moved = roll(received[block, 128:], 16 * block - 16 * quarter)
            tile = jnp.where(lane // 16 == block, moved, tile)
        planes.append(tile)
    planes = jnp.concatenate(planes, axis=0)
    edge = jnp.concatenate(
        [jnp.where(lanes(planes) % 8 == y, planes, 0.0) for y in range(8)], axis=0
    )
    main = jnp.concatenate(
        [jnp.concatenate(lower, axis=1), jnp.concatenate(upper, axis=1)], axis=0
    )
    image = data_dot(jnp.concatenate([main, edge], axis=1), table)
    for y in range(8):
        out[:, y, :] = image[y * 32 : y * 32 + 32, :] + prior[:, y, :] * volume[:, y, :]
    total = jnp.sum(received[:, 128:, 127:].reshape(GX * 8, 1)) / 8.0
    curvature[0] = total / float(M) ** 3


def whole():
    return pl.BlockSpec(memory_space=pltpu.VMEM)


def anywhere():
    return pl.BlockSpec(memory_space=pl.ANY)


def in_hbm():
    return pl.BlockSpec(memory_space=pltpu.HBM)


def params(limit=VM):
    return pltpu.CompilerParams(vmem_limit_bytes=limit * 1024 * 1024)


def cost(micros):
    return pl.CostEstimate(flops=int(micros * 1e9), bytes_accessed=8 << 20, transcendentals=0)


def f32(*shape):
    return jax.ShapeDtypeStruct(shape, jnp.float32)


def mirror(value):
    pairs = [(GA - 1 - group, group) for group in range(GA)]
    return lax.ppermute(value, ("gy", "gz"), pairs)


def onward(value):
    return lax.ppermute(value, ("gy", "gz"), [(group, (group + 1) % GA) for group in range(GA)])


def reflect(value):
    count = GX * GA
    return lax.ppermute(value, AXES, [(count - 1 - at, at) for at in range(count)])


def opposite(value):
    return lax.ppermute(value, "gx", [(GX - 1 - block, block) for block in range(GX)])


def local(volume, prior_weight, kernel):
    late, early = pl.pallas_call(
        turn_kernel,
        out_shape=(f32(LATE, HALF, N), f32(EARLY + 1, HALF, N)),
        in_specs=[in_hbm()],
        out_specs=(whole(), whole()),
        scratch_shapes=[pltpu.VMEM((16, HALF, N), jnp.float32), pltpu.SemaphoreType.DMA((16,))],
        compiler_params=params(63),
        cost_estimate=cost(TURN_COST),
        name="turn",
    )(kernel)
    plane = mirror(late)
    near = reflect(early)
    rim = onward(near[EARLY:])
    base, partial = pl.pallas_call(
        own_kernel,
        out_shape=(f32(N, 1152), f32(8, 128)),
        in_specs=[whole()] * 3,
        out_specs=(whole(), whole()),
        compiler_params=params(),
        cost_estimate=cost(OWN_COST),
        name="own_weights",
    )(kernel, volume, prior_weight)
    sent = pl.pallas_call(
        z_forward_kernel,
        out_shape=f32(GX, 136, 128),
        in_specs=[in_hbm()] * 2,
        out_specs=whole(),
        scratch_shapes=[
            pltpu.VMEM((32, 8, M), jnp.float32),
            pltpu.VMEM((2 * M, 640), BF),
            pltpu.SemaphoreType.DMA((8,)),
        ],
        compiler_params=params(63),
        name="z_forward",
    )(volume, z_forward_table())
    got = lax.all_to_all(sent, "gx", split_axis=0, concat_axis=0, tiled=True)
    far = opposite(plane)
    sent = pl.pallas_call(
        x_forward_kernel,
        out_shape=f32(GA, 9, 8, 128),
        in_specs=[whole(), anywhere(), whole()],
        out_specs=whole(),
        compiler_params=params(),
        name="x_forward",
    )(got, plane, forward_table())
    got = lax.all_to_all(sent, ("gy", "gz"), split_axis=0, concat_axis=0, tiled=True)
    spectrum = pl.pallas_call(
        y_forward_kernel,
        out_shape=f32(N, 1152),
        in_specs=[whole()] * 2,
        out_specs=whole(),
        compiler_params=params(),
        cost_estimate=cost(FORWARD_COST),
        name="y_forward",
    )(got.reshape(GA * 72, 128), forward_table())
    sent = pl.pallas_call(
        y_inverse_kernel,
        out_shape=f32(GA, 8, 1152),
        in_specs=[whole()] * 7,
        out_specs=whole(),
        compiler_params=params(),
        name="y_inverse",
    )(spectrum, base, far, near, rim, partial, inverse_table())
    got = lax.all_to_all(sent, ("gy", "gz"), split_axis=0, concat_axis=0, tiled=True)
    sent = pl.pallas_call(
        x_inverse_kernel,
        out_shape=f32(GX, 136, 128),
        in_specs=[whole()] * 3,
        out_specs=whole(),
        compiler_params=params(),
        name="x_inverse",
    )(got, x_inverse_table(), inverse_table())
    got = lax.all_to_all(sent, "gx", split_axis=0, concat_axis=0, tiled=True)
    product, curvature = pl.pallas_call(
        z_inverse_kernel,
        out_shape=(f32(32, 8, M), f32(1)),
        in_specs=[whole()] * 4,
        out_specs=(whole(), pl.BlockSpec(memory_space=pltpu.SMEM)),
        compiler_params=params(),
        name="z_inverse",
    )(got, volume, prior_weight, z_inverse_table())
    return product, curvature


def solution(mesh):
    return jax.shard_map(
        local,
        mesh=mesh,
        in_specs=(
            P("gx", ("gy", "gz"), None),
            P("gx", ("gy", "gz"), None),
            P(("gy", "gz"), "gx", None),
        ),
        out_specs=(P("gx", ("gy", "gz"), None), P()),
        check_vma=False,
    )
```

```python
import math

import jax
import jax.numpy as jnp
import ml_dtypes
import numpy as np
from jax import lax
from jax.experimental import pallas as pl
from jax.experimental.pallas import tpu as pltpu
from jax.sharding import PartitionSpec as P

M = 256
N = 512
GX = 8
GA = 32
HALF = 32
EARLY = 7
LATE = 15 - EARLY
OWN_COST = 20
TURN_COST = 8
FORWARD_COST = 5
AXES = ("gx", "gy", "gz")
VM = 32
BF = jnp.bfloat16


def trig(rows, cols):
    product = np.outer(np.asarray(rows), np.asarray(cols)) % N
    angle = product * (2.0 * math.pi / N)
    return np.cos(angle), np.sin(angle)


def halves(table):
    table = np.asarray(table, np.float32)
    high = table.astype(ml_dtypes.bfloat16)
    low = (table - high.astype(np.float32)).astype(ml_dtypes.bfloat16)
    return high, low


def z_forward_table():
    cosine, sine = trig(np.arange(M), np.arange(N))
    stacked = np.stack([cosine, -sine], axis=0).reshape(2, M, GX // 2, 2, 64)
    main = stacked[..., :HALF].transpose(1, 2, 0, 3, 4).reshape(M, GX * 64)
    edge = stacked[..., HALF].transpose(1, 2, 3, 0).reshape(M, GX * 2)
    return np.concatenate(halves(np.concatenate([main, np.repeat(edge, 8, axis=1)], axis=1)), axis=0)


def z_inverse_table():
    cosine, sine = trig(np.arange(N), np.arange(M))
    stacked = np.stack([cosine, -sine], axis=0).reshape(2, GX // 2, 2, 64, M)
    main = stacked[:, :, :, :HALF].transpose(1, 0, 2, 3, 4).reshape(GX * 64, M)
    edge = stacked[:, :, :, HALF].transpose(1, 2, 0, 3).reshape(GX * 2, M)
    return stack_right(np.concatenate([main, np.repeat(edge, 8, axis=0)], axis=0) / float(N) ** 3)


def forward_table():
    cosine, sine = trig(np.arange(N), np.arange(M))
    return stack_left(np.concatenate([cosine, sine], axis=1))


def inverse_table():
    cosine, sine = trig(np.arange(M), np.arange(N))
    return stack_left(np.concatenate([cosine, sine], axis=1))


def x_inverse_table():
    order = np.arange(N).reshape(GA, 16).T.reshape(-1)
    cosine, sine = trig(np.arange(M), order)
    return stack_left(np.concatenate([cosine, sine], axis=1))


def split(value):
    high = value.astype(BF)
    low = (value - high.astype(jnp.float32)).astype(BF)
    return high, low


def dot(left, right):
    return jnp.dot(left, right, preferred_element_type=jnp.float32)


def stack_left(table):
    return np.concatenate(halves(table), axis=0)


def stack_right(table):
    high, low = halves(table)
    return np.concatenate([high, low, high], axis=0)


def table_dot(table, data):
    high, low = split(data)
    count = table.shape[0] // 2
    wide = dot(table[...], high)
    return wide[:count] + (wide[count:] + dot(table[:count], low))


def data_dot(data, table):
    high, low = split(data)
    return dot(jnp.concatenate([high, high, low], axis=1), table[...])


def rotated(value, sign):
    lane = lax.broadcasted_iota(jnp.int32, value.shape, 1)
    swapped = pltpu.roll(value, 64, 1)
    return jnp.where(lane < 64, sign * swapped, -sign * swapped)


def fold(value):
    rows, cols = value.shape
    total = jnp.sum(value.reshape(rows // 8, 8, cols), axis=0)
    parts = [total[:, at : at + 128] for at in range(0, cols, 128)]
    return sum(parts[1:], parts[0])


def lanes(value):
    return lax.broadcasted_iota(jnp.int32, value.shape, value.ndim - 1)


def roll(value, shift):
    shift = shift % 128
    return value if shift == 0 else pltpu.roll(value, shift, value.ndim - 1)


def exchange(first, second):
    even = (lanes(first) & HALF) == 0
    low = jnp.where(even, first, roll(second, HALF))
    high = jnp.where(even, roll(first, -HALF), second)
    return low, high


def complex_dot(table, tiles, sign):
    real = jnp.concatenate(tiles, axis=1)
    turned = jnp.concatenate([rotated(tile, sign) for tile in tiles], axis=1)
    return table_dot(table, jnp.concatenate([real, turned], axis=0))


def z_forward_kernel(volume, table, out, field, held, sems):
    copies = []
    for part in range(4):
        place = pl.ds(part * 8, 8)
        copies.append(pltpu.make_async_copy(volume.at[place], field.at[place], sems.at[part]))
    for part in range(4):
        place = pl.ds(part * 128, 128)
        copies.append(pltpu.make_async_copy(table.at[place], held.at[place], sems.at[4 + part]))
    for copy in copies:
        copy.start()
    for copy in copies[:4]:
        copy.wait()
    high, low = split(jnp.concatenate([field[:, y, :] for y in range(8)], axis=0))
    for copy in copies[4:]:
        copy.wait()
    res = dot(jnp.concatenate([high, low], axis=0), held[:M])
    res = res[:M] + (res[M:] + dot(high, held[M:]))
    for pair in range(GX // 2):
        tile = res[:, pair * 128 : pair * 128 + 128]
        first, second = exchange(tile[:128], tile[128:])
        out[2 * pair, :128] = first
        out[2 * pair + 1, :128] = second
    edge = res[:, GX * 64 :]
    lane = lax.broadcasted_iota(jnp.int32, (32, 128), 1)
    planes = jnp.zeros((32, 128), jnp.float32)
    for y in range(8):
        planes = jnp.where(lane % 8 == y, edge[y * 32 : y * 32 + 32], planes)
    lane = lax.broadcasted_iota(jnp.int32, (8, 128), 1)
    for block in range(GX):
        tile = jnp.zeros((8, 128), jnp.float32)
        for quarter in range(4):
            moved = roll(planes[quarter * 8 : quarter * 8 + 8], 16 * quarter - 16 * block)
            tile = jnp.where(lane // 16 == quarter, moved, tile)
        out[block, 128:] = tile


def x_forward_kernel(received, held, table, out):
    for pair in range(2):
        tiles = [
            received[:, y * 32 : y * 32 + 32, :].reshape(M, 128) for y in (2 * pair, 2 * pair + 1)
        ]
        res = complex_dot(table, tiles, 1.0)
        for at in range(2):
            blocks = res[:, at * 128 : at * 128 + 128].reshape(GA, 2, 8, 128)
            first, second = exchange(blocks[:, 0].reshape(M, 128), blocks[:, 1].reshape(M, 128))
            out[:, 2 * pair + at] = first.reshape(GA, 8, 128)
            out[:, 2 * pair + at + 4] = second.reshape(GA, 8, 128)
    lane = lax.broadcasted_iota(jnp.int32, (8, 128), 1)
    rows = []
    for block in range(GX):
        tile = received[block, 128:, :]
        for quarter in range(4):
            real = roll(tile, -16 * quarter)
            imag = roll(tile, 56 - 16 * quarter)
            rows.append(jnp.where(lane < 64, real, imag))
    res = complex_dot(table, [jnp.concatenate(rows, axis=0)], 1.0).T
    for group in range(GA):
        cols = slice(group // 8 * 128, group // 8 * 128 + 128)
        shift = -16 * (group % 8)
        out[group, 8] = jnp.where(
            lane < 64, roll(res[0:8, cols], shift), roll(res[64:72, cols], shift + 64)
        )


def doubled(tile):
    first, second = tile[:, :64], tile[:, 64:]
    return jnp.concatenate([first, first, second, second], axis=1)


def pair_order(pair):
    return 2 * pair, 2 * pair + 8, 2 * pair + 1, 2 * pair + 9


def flipped(rows):
    shape = (128, 128)
    at, source = (lax.broadcasted_iota(jnp.int32, shape, axis) for axis in (0, 1))
    planes = (at // HALF == source // HALF) & (at % HALF + source % HALF == HALF)
    planes = jnp.where(planes, 1.0, 0.0).astype(BF)
    at, source = (lax.broadcasted_iota(jnp.int32, (N, N), axis) for axis in (0, 1))
    flip = jnp.where((at + source) % N == 0, 1.0, 0.0).astype(BF)
    count = rows.shape[0]
    high, low = [], []
    for first in range(0, count, 128):
        block = dot(planes, jnp.concatenate(split(rows[first : first + 128]), axis=1))
        upper, lower = split(block[:, :N] + block[:, N:])
        high.append(upper)
        low.append(lower)
    res = dot(jnp.concatenate(high + low, axis=0), flip)
    return res[:count] + res[count:]


def turn_kernel(own, late, early, rows, sems):
    copies = [
        pltpu.make_async_copy(own.at[k, pl.ds(HALF, HALF)], rows.at[k], sems.at[k])
        for k in range(16)
    ]
    for copy in copies:
        copy.start()
    for copy in copies:
        copy.wait()
    res = flipped(jnp.concatenate([rows[(16 - k) % 16] for k in range(1, 17)], axis=0))
    res = res.reshape(16, HALF, N)
    early[:EARLY] = res[:EARLY]
    early[EARLY:] = res[15:]
    late[...] = res[EARLY:15]


def own_kernel(own, volume, prior, out, partial):
    field = volume[...]
    partial[...] = fold((prior[...] * field * field).reshape(M, M))
    for pair in range(4):
        rows = jnp.concatenate([own[k, :HALF] for k in pair_order(pair)], axis=0)
        out[:, pair * 256 : pair * 256 + 256] = doubled(rows.T)
    edge = jnp.concatenate([own[:, HALF, :], jnp.zeros((48, N), jnp.float32)] * 2, axis=0)
    out[:, 1024:] = edge.T


def y_forward_kernel(received, table, out):
    for pair in range(4):
        tiles = []
        for at in range(2):
            rows = [
                received[pl.ds(group * 72 + pair * 2 + at, 8, stride=8), :] for group in range(GA)
            ]
            tiles.append(jnp.concatenate(rows, axis=0))
        out[:, pair * 256 : pair * 256 + 256] = complex_dot(table, tiles, 1.0)
    rows = [received[group * 72 + 64 : group * 72 + 72, :] for group in range(GA)]
    out[:, 1024:] = complex_dot(table, [jnp.concatenate(rows, axis=0)], 1.0)


def y_inverse_kernel(spectrum, base, far, near, rim, partial, table, out):
    def extra(pair):
        rows = [
            far[k - EARLY - 1] if k > EARLY else near[k - 1] if k else rim[0]
            for k in pair_order(pair)
        ]
        return doubled(jnp.concatenate(rows, axis=0).T)

    total = partial[...]
    for pair in range(5):
        place = slice(pair * 256, min(pair * 256 + 256, 1152))
        scale = base[:, place]
        if pair < 4:
            scale += extra(pair)
        values = spectrum[:, place]
        weighted = values * scale
        total += fold(weighted * values) * (1.0 / float(N) ** 3)
        cols = [weighted[:, at : at + 128] for at in range(0, values.shape[1], 128)]
        res = complex_dot(table, cols, -1.0)
        if pair == 4:
            res = jnp.where(lanes(res) < 96, res, jnp.sum(total))
        out[:, :, place] = res.reshape(GA, 8, res.shape[1])


def x_inverse_kernel(received, table, plain, out):
    for pair in range(2):
        tiles = []
        for y in (2 * pair, 2 * pair + 1):
            first, second = (
                jnp.concatenate(
                    [received[:, at, k * 128 : k * 128 + 128] for k in range(8)], axis=0
                )
                for at in (y, y + 4)
            )
            tiles.append(jnp.concatenate(exchange(first, second), axis=0))
        res = complex_dot(table, tiles, -1.0)
        for at in range(2):
            y = 2 * pair + at
            out[:, y * 32 : y * 32 + 32, :] = res[:, at * 128 : at * 128 + 128].reshape(GX, 32, 128)
    lane = lax.broadcasted_iota(jnp.int32, (8, 128), 1)
    real, imag = [], []
    count = jnp.zeros((1, 1), jnp.float32)
    for four in range(4):
        real_tile = jnp.zeros((8, 128), jnp.float32)
        imag_tile = real_tile
        for at in range(8):
            tile = received[four * 8 + at, :, 1024:]
            count += tile[:1, 127:]
            here = lane // 16 == at
            real_tile = jnp.where(here, roll(tile, 16 * at), real_tile)
            imag_tile = jnp.where(here, roll(tile, 16 * at - 64), imag_tile)
        real.append(real_tile)
        imag.append(imag_tile)
    blank = jnp.zeros((56, N), jnp.float32)
    stacked = jnp.concatenate(
        [jnp.concatenate(real, axis=1), blank, jnp.concatenate(imag, axis=1), blank], axis=0
    )
    res = complex_dot(plain, [stacked.T], -1.0)
    for block in range(GX):
        tile = jnp.broadcast_to(count, (8, 128))
        for quarter in range(4):
            part = res[block * 32 + quarter * 8 : block * 32 + quarter * 8 + 8]
            tile = jnp.where(lane // 8 == 2 * quarter, roll(part, 16 * quarter), tile)
            tile = jnp.where(lane // 8 == 2 * quarter + 1, roll(part, 16 * quarter - 56), tile)
        out[block, 128:] = tile


def z_inverse_kernel(received, volume, prior, table, out, curvature):
    lower, upper = [], []
    for pair in range(GX // 2):
        first, second = exchange(received[2 * pair, :128], received[2 * pair + 1, :128])
        lower.append(first)
        upper.append(second)
    lane = lax.broadcasted_iota(jnp.int32, (8, 128), 1)
    planes = []
    for quarter in range(4):
        tile = jnp.zeros((8, 128), jnp.float32)
        for block in range(GX):
            moved = roll(received[block, 128:], 16 * block - 16 * quarter)
            tile = jnp.where(lane // 16 == block, moved, tile)
        planes.append(tile)
    planes = jnp.concatenate(planes, axis=0)
    edge = jnp.concatenate(
        [jnp.where(lanes(planes) % 8 == y, planes, 0.0) for y in range(8)], axis=0
    )
    main = jnp.concatenate(
        [jnp.concatenate(lower, axis=1), jnp.concatenate(upper, axis=1)], axis=0
    )
    image = data_dot(jnp.concatenate([main, edge], axis=1), table)
    for y in range(8):
        out[:, y, :] = image[y * 32 : y * 32 + 32, :] + prior[:, y, :] * volume[:, y, :]
    total = jnp.sum(received[:, 128:, 127:].reshape(GX * 8, 1)) / 8.0
    curvature[0] = total / float(M) ** 3


def whole():
    return pl.BlockSpec(memory_space=pltpu.VMEM)


def anywhere():
    return pl.BlockSpec(memory_space=pl.ANY)


def in_hbm():
    return pl.BlockSpec(memory_space=pltpu.HBM)


def params(limit=VM):
    return pltpu.CompilerParams(vmem_limit_bytes=limit * 1024 * 1024)


def cost(micros):
    return pl.CostEstimate(flops=int(micros * 1e9), bytes_accessed=8 << 20, transcendentals=0)


def f32(*shape):
    return jax.ShapeDtypeStruct(shape, jnp.float32)


def mirror(value):
    pairs = [(GA - 1 - group, group) for group in range(GA)]
    return lax.ppermute(value, ("gy", "gz"), pairs)


def onward(value):
    return lax.ppermute(value, ("gy", "gz"), [(group, (group + 1) % GA) for group in range(GA)])


def reflect(value):
    count = GX * GA
    return lax.ppermute(value, AXES, [(count - 1 - at, at) for at in range(count)])


def opposite(value):
    return lax.ppermute(value, "gx", [(GX - 1 - block, block) for block in range(GX)])


def local(volume, prior_weight, kernel):
    late, early = pl.pallas_call(
        turn_kernel,
        out_shape=(f32(LATE, HALF, N), f32(EARLY + 1, HALF, N)),
        in_specs=[in_hbm()],
        out_specs=(whole(), whole()),
        scratch_shapes=[pltpu.VMEM((16, HALF, N), jnp.float32), pltpu.SemaphoreType.DMA((16,))],
        compiler_params=params(63),
        cost_estimate=cost(TURN_COST),
        name="turn",
    )(kernel)
    plane = mirror(late)
    near = reflect(early)
    rim = onward(near[EARLY:])
    base, partial = pl.pallas_call(
        own_kernel,
        out_shape=(f32(N, 1152), f32(8, 128)),
        in_specs=[whole()] * 3,
        out_specs=(whole(), whole()),
        compiler_params=params(),
        cost_estimate=cost(OWN_COST),
        name="own_weights",
    )(kernel, volume, prior_weight)
    sent = pl.pallas_call(
        z_forward_kernel,
        out_shape=f32(GX, 136, 128),
        in_specs=[in_hbm()] * 2,
        out_specs=whole(),
        scratch_shapes=[
            pltpu.VMEM((32, 8, M), jnp.float32),
            pltpu.VMEM((2 * M, 640), BF),
            pltpu.SemaphoreType.DMA((8,)),
        ],
        compiler_params=params(63),
        name="z_forward",
    )(volume, z_forward_table())
    got = lax.all_to_all(sent, "gx", split_axis=0, concat_axis=0, tiled=True)
    far = opposite(plane)
    sent = pl.pallas_call(
        x_forward_kernel,
        out_shape=f32(GA, 9, 8, 128),
        in_specs=[whole(), anywhere(), whole()],
        out_specs=whole(),
        compiler_params=params(),
        name="x_forward",
    )(got, plane, forward_table())
    got = lax.all_to_all(sent, ("gy", "gz"), split_axis=0, concat_axis=0, tiled=True)
    spectrum = pl.pallas_call(
        y_forward_kernel,
        out_shape=f32(N, 1152),
        in_specs=[whole()] * 2,
        out_specs=whole(),
        compiler_params=params(),
        cost_estimate=cost(FORWARD_COST),
        name="y_forward",
    )(got.reshape(GA * 72, 128), forward_table())
    sent = pl.pallas_call(
        y_inverse_kernel,
        out_shape=f32(GA, 8, 1152),
        in_specs=[whole()] * 7,
        out_specs=whole(),
        compiler_params=params(),
        name="y_inverse",
    )(spectrum, base, far, near, rim, partial, inverse_table())
    got = lax.all_to_all(sent, ("gy", "gz"), split_axis=0, concat_axis=0, tiled=True)
    sent = pl.pallas_call(
        x_inverse_kernel,
        out_shape=f32(GX, 136, 128),
        in_specs=[whole()] * 3,
        out_specs=whole(),
        compiler_params=params(),
        name="x_inverse",
    )(got, x_inverse_table(), inverse_table())
    got = lax.all_to_all(sent, "gx", split_axis=0, concat_axis=0, tiled=True)
    product, curvature = pl.pallas_call(
        z_inverse_kernel,
        out_shape=(f32(32, 8, M), f32(1)),
        in_specs=[whole()] * 4,
        out_specs=(whole(), pl.BlockSpec(memory_space=pltpu.SMEM)),
        compiler_params=params(),
        name="z_inverse",
    )(got, volume, prior_weight, z_inverse_table())
    return product, curvature


def solution(mesh):
    return jax.shard_map(
        local,
        mesh=mesh,
        in_specs=(
            P("gx", ("gy", "gz"), None),
            P("gx", ("gy", "gz"), None),
            P(("gy", "gz"), "gx", None),
        ),
        out_specs=(P("gx", ("gy", "gz"), None), P()),
        check_vma=False,
    )
```
